256 devices in a mesh: tile: 2 (over core), ta: 16 (over y, x), gx: 8 (over z).
Axes of the slice: x: 4, y: 4, z: 8, core: 2. Of those that a mesh axis runs over, the one named last changes fastest.
Arguments:
- field: float32 [8192, 4096], P(('tile', 'ta'), 'gx'), parts along dimension 0, may hold values from -7.5 to 7.5
- time_period: float32 [2], P('tile'), parts along dimension 0, may hold values from 8192 to 16384
- space_period: float32 [2], P('tile'), parts along dimension 0, may hold values from 10240 to 16384
Outputs:
- updated_field: float32 [8192, 4096], P(('tile', 'ta'), 'gx'), parts along dimension 0
- residual: float32 [8192, 4096], P(('tile', 'ta'), 'gx'), parts along dimension 0
The draws below stay inside these ranges and needn't reach their ends.
There are 2 independent parts, one for each index of `tile`. The reference program is written for one: setup_inputs(seed, part) draws one part's arguments, and reference() takes and returns one part's arrays. A program takes and returns all parts, laid end to end along the dimension named above; each array names one. Nothing has to cross between parts.
All inputs are finite; a program needn't handle non-finite values.
Results may differ from the reference program's by a relative error of at most 0.000092.
Values sent between devices are 32-bit elements; how exact they have to be, the bound alone decides.
No kernel may reach another device: no remote copies, remote signals or barrier semaphores. Data moves between devices by JAX's collectives and lax.ppermute only.
A program may use at most 64 MiB of HBM per device.

```python
import math
import jax
import jax.numpy as jnp

NT = 4096
NX = 4096


def draw_field(key, part):
    key = jax.random.fold_in(key, 11)
    time_frac = jnp.arange(NT, dtype=jnp.float32)[:, None] / NT
    rough = jax.random.truncated_normal(key, -4.0, 4.0, (NT, NX), jnp.float32)
    scale = 0.6 * jnp.exp(math.log(3.0) * time_frac)
    return scale * rough


def setup_inputs(seed: int = 0, part: int = 0) -> dict:
    key_list = jax.random.split(jax.random.key(seed), 4)
    part_splits = jax.random.split(jax.random.fold_in(key_list[3], part), 4)
    field = draw_field(jax.random.fold_in(jax.random.fold_in(key_list[3], part), 71), part)
    time_period = jnp.clip(jax.random.uniform(part_splits[1], (1,), jnp.float32, 8192.0, 16384.0), 8192.0, 16384.0)
    space_period = jnp.clip(jax.random.uniform(part_splits[2], (1,), jnp.float32, 10240.0, 16384.0), 10240.0, 16384.0)
    return dict(field=field, time_period=time_period, space_period=space_period)


def mode_numbers(count):
    position = jnp.arange(count, dtype=jnp.int32)
    signed = jnp.where(position < count // 2, position, position - count)
    odd = jnp.where(position == count // 2, 0, signed)
    return signed, odd


def reference(field, time_period, space_period):
    float_type = field.dtype
    two_pi = 2.0 * math.pi
    time_signed, time_odd = mode_numbers(NT)
    space_signed, space_odd = mode_numbers(NX)
    omega = (two_pi * time_odd.astype(float_type) / time_period[0])[:, None]
    wave = two_pi * space_signed.astype(float_type) / space_period[0]
    wave_odd = (two_pi * space_odd.astype(float_type) / space_period[0])[None, :]
    even_part = (wave ** 4 - wave ** 2)[None, :]
    spectrum = jnp.fft.fft2(field)
    linear = jnp.real(jnp.fft.ifft2((1j * omega + even_part) * spectrum)).astype(float_type)
    slope = jnp.real(jnp.fft.ifft2((1j * wave_odd) * spectrum)).astype(float_type)
    residual = linear + field * slope
    residual_spectrum = jnp.fft.fft2(residual)
    adjoint = jnp.real(jnp.fft.ifft2((-1j * omega + even_part) * residual_spectrum)).astype(float_type)
    residual_slope = jnp.real(jnp.fft.ifft2((1j * wave_odd) * residual_spectrum)).astype(float_type)
    gradient = adjoint - field * residual_slope
    cost = 0.5 * jnp.sum(residual * residual)
    grad_norm = jnp.sum(gradient * gradient)
    step_size = cost / (grad_norm + 1e-6)
    return field - step_size * gradient, residual
```

```python
import math

import jax
import jax.numpy as jnp
import ml_dtypes
import numpy as np
from jax import lax
from jax.experimental import pallas as pl
from jax.experimental.pallas import tpu as pltpu
from jax.sharding import PartitionSpec as P

TWO_PI = 2.0 * math.pi
GRAD_EPS = 1e-06
LEN = 4096
RADIX = 16
SUB = 256
PARTS = 3
GROUP = 4
VMEM_LIMIT = 24 * 1024 * 1024


def np_parts(values):
    rest = np.asarray(values, np.float64)
    parts = []
    for _ in range(PARTS):
        part = rest.astype(np.float32).astype(ml_dtypes.bfloat16)
        parts.append(part)
        rest = rest - part.astype(np.float64)
    return parts


def np_tables():
    j = np.arange(SUB)
    angle = TWO_PI * (np.outer(j, j) % SUB) / SUB
    dft = np.stack(np_parts(np.cos(angle)) + np_parts(np.sin(angle)))
    k1 = np.arange(RADIX)
    twist = TWO_PI * np.outer(k1, j) / LEN
    mode = k1[:, None] + RADIX * j[None, :]
    signed = np.where(mode < LEN // 2, mode, mode - LEN)
    odd = np.where(mode == LEN // 2, 0, signed)
    small = np.stack([np.cos(twist), np.sin(twist), signed, odd]).astype(np.float32)
    return dft, small


def cadd(a, b):
    return (a[0] + b[0], a[1] + b[1])


def csub(a, b):
    return (a[0] - b[0], a[1] - b[1])


def dft4(x, sign):
    s = cadd(x[0], x[2])
    d = csub(x[0], x[2])
    t = cadd(x[1], x[3])
    e = csub(x[1], x[3])
    if sign < 0:
        ie = (e[1], -e[0])
    else:
        ie = (-e[1], e[0])
    return [cadd(s, t), cadd(d, ie), csub(s, t), csub(d, ie)]


def crot(x, turns, sign):
    if turns == 0:
        return x
    if turns == 4:
        return (x[1], -x[0]) if sign < 0 else (-x[1], x[0])
    c = math.cos(TWO_PI * turns / 16)
    s = sign * math.sin(TWO_PI * turns / 16)
    if turns == 2:
        return ((x[0] - sign * x[1]) * c, (x[1] + sign * x[0]) * c)
    if turns == 6:
        return ((x[0] + sign * x[1]) * c, (x[1] - sign * x[0]) * c)
    return (x[0] * c - x[1] * s, x[0] * s + x[1] * c)


def dft16(x, sign):
    out = [None] * 16
    rows = []
    for n2 in range(4):
        y = dft4([x[4 * n1 + n2] for n1 in range(4)], sign)
        rows.append([crot(y[k1], n2 * k1, sign) for k1 in range(4)])
    for k1 in range(4):
        z = dft4([rows[n2][k1] for n2 in range(4)], sign)
        for k2 in range(4):
            out[k1 + 4 * k2] = z[k2]
    return out


def split(values):
    parts = []
    rest = values
    for step in range(PARTS):
        part = rest.astype(jnp.bfloat16)
        parts.append(part)
        if step < PARTS - 1:
            rest = rest - part.astype(jnp.float32)
    return parts


def product(parts, table, first):
    total = None
    for order in reversed(range(PARTS)):
        for i in range(order + 1):
            term = jnp.dot(
                parts[i], table[first + order - i], preferred_element_type=jnp.float32
            )
            total = term if total is None else total + term
    return total


def transform(get, put, outputs, symbol, dft_ref, small_ref, a_ref, b_ref):
    for lane in range(2):
        lanes = slice(lane * 128, lane * 128 + 128)
        planes = dft16([get(m, lanes) for m in range(RADIX)], -1)
        for k1 in range(RADIX):
            re, im = planes[k1]
            if k1:
                c = small_ref[0, k1 : k1 + 1, lanes]
                s = small_ref[1, k1 : k1 + 1, lanes]
                re, im = re * c + im * s, im * c - re * s
            a_ref[k1, 0:16, lanes] = re
            a_ref[k1, 16:32, lanes] = im
    rows = GROUP * 16
    for group in range(RADIX // GROUP):
        ks = slice(group * GROUP, (group + 1) * GROUP)
        left = split(a_ref[ks].reshape(GROUP * 32, SUB))
        with_cos = product(left, dft_ref, 0).reshape(GROUP, 2, 16, SUB)
        with_sin = product(left, dft_ref, PARTS).reshape(GROUP, 2, 16, SUB)
        re = with_cos[:, 0] + with_sin[:, 1]
        im = with_cos[:, 1] - with_sin[:, 0]
        for o in range(outputs):
            sre, sim = symbol(o, ks, re, im)
            left = split(jnp.concatenate([sre, sim], axis=1).reshape(GROUP * 32, SUB))
            with_cos = product(left, dft_ref, 0).reshape(GROUP, 2, 16, SUB)
            with_sin = product(left, dft_ref, PARTS).reshape(GROUP, 2, 16, SUB)
            re2 = with_cos[:, 0] - with_sin[:, 1]
            im2 = with_cos[:, 1] + with_sin[:, 0]
            c = small_ref[0, ks][:, None, :]
            s = small_ref[1, ks][:, None, :]
            b_ref[o, ks, 0:16] = re2 * c - im2 * s
            b_ref[o, ks, 16:32] = im2 * c + re2 * s
    for lane in range(2):
        lanes = slice(lane * 128, lane * 128 + 128)
        outs = []
        for o in range(outputs):
            planes = [(b_ref[o, k, 0:16, lanes], b_ref[o, k, 16:32, lanes]) for k in range(RADIX)]
            outs.append(dft16(planes, 1))
        for m in range(RADIX):
            put(m, lanes, [outs[o][m] for o in range(outputs)])


def space_symbol(scale, small_ref):
    def symbol(o, ks, re, im):
        if o == 0:
            wave = small_ref[2, ks] * scale
            square = wave * wave
            even = ((square * square - square) * (1.0 / LEN))[:, None, :]
            return re * even, im * even
        odd = (small_ref[3, ks] * (scale * (1.0 / LEN)))[:, None, :]
        return -im * odd, re * odd

    return symbol


def time_symbol(scale, small_ref):
    def symbol(o, ks, re, im):
        odd = (small_ref[3, ks] * (scale * (1.0 / LEN)))[:, None, :]
        return -im * odd, re * odd

    return symbol


def space_at(m, lanes):
    start = (m % 2) * 256 + lanes.start
    return m // 2, slice(start, start + 128)


def blocks4(tiles):
    lane = lax.broadcasted_iota(jnp.int32, tiles[0].shape, len(tiles[0].shape) - 1)
    axis = len(tiles[0].shape) - 1
    low_half = lane < 64
    even = (lane // 32) % 2 == 0

    def swap(x, y, shift, mask):
        first = jnp.where(mask, x, pltpu.roll(y, shift, axis))
        second = jnp.where(mask, pltpu.roll(x, 128 - shift, axis), y)
        return first, second

    t0, t2 = swap(tiles[0], tiles[2], 64, low_half)
    t1, t3 = swap(tiles[1], tiles[3], 64, low_half)
    t0, t1 = swap(t0, t1, 32, even)
    t2, t3 = swap(t2, t3, 32, even)
    return [t0, t1, t2, t3]


def turn_kernel(u_ref, out_ref):
    for h in range(2):
        for a in range(4):
            tile = u_ref[h * 128 : h * 128 + 128, a * 128 : a * 128 + 128].T
            out_ref[:, a * 8 : a * 8 + 8, h * 128 : h * 128 + 128] = tile.reshape(16, 8, 128)


def space_first_kernel(scale_ref, u_ref, dft_ref, small_ref, out_ref, p_ref, a_ref, b_ref):
    def get(m, lanes):
        g, cols = space_at(m, lanes)
        return (u_ref[g, 0:16, cols], u_ref[g, 16:32, cols])

    def put(m, lanes, values):
        g, cols = space_at(m, lanes)
        for half in range(2):
            rows = slice(16 * half, 16 * half + 16)
            p_ref[g, rows, cols] = values[0][half] + u_ref[g, rows, cols] * values[1][half]

    transform(get, put, 2, space_symbol(scale_ref[0], small_ref), dft_ref, small_ref, a_ref, b_ref)
    for g in range(8):
        stack = jnp.concatenate([p_ref[g, :, a * 128 : a * 128 + 128] for a in range(4)], axis=0)
        turned = stack.T.reshape(16, 8, 128)
        for owner in range(16):
            out_ref[owner * 8 + g] = turned[owner]


def time_first_kernel(scale_ref, u_ref, dft_ref, small_ref, out_ref, q_ref, a_ref, b_ref):
    def get(m, lanes):
        return (u_ref[m, 0:16, lanes], u_ref[m, 16:32, lanes])

    def put(m, lanes, values):
        q_ref[m, 0:16, lanes] = values[0][0]
        q_ref[m, 16:32, lanes] = values[0][1]

    transform(get, put, 1, time_symbol(scale_ref[0], small_ref), dft_ref, small_ref, a_ref, b_ref)
    for m in range(16):
        for h in range(2):
            tiles = blocks4(
                [q_ref[m, 8 * a : 8 * a + 8, h * 128 : h * 128 + 128] for a in range(4)]
            )
            for k in range(4):
                out_ref[m * 8 + 4 * h + k] = tiles[k]


def time_second_kernel(
    scale_ref, q_ref, recv_ref, dft_ref, small_ref, out_ref, cost_ref, a_ref, b_ref
):
    total = jnp.zeros((8, 128), jnp.float32)
    for m in range(16):
        for h in range(2):
            tiles = blocks4([recv_ref[m * 8 + 4 * h + k, 0] for k in range(4)])
            for a in range(4):
                rows = slice(8 * a, 8 * a + 8)
                cols = slice(h * 128, h * 128 + 128)
                value = q_ref[m, rows, cols] + tiles[a]
                out_ref[m, 0, rows, cols] = value
                total = total + value * value
    cost_ref[...] = total * 0.5

    def get(m, lanes):
        return (out_ref[m, 0, 0:16, lanes], out_ref[m, 0, 16:32, lanes])

    def put(m, lanes, values):
        out_ref[m, 1, 0:16, lanes] = -values[0][0]
        out_ref[m, 1, 16:32, lanes] = -values[0][1]

    transform(get, put, 1, time_symbol(scale_ref[0], small_ref), dft_ref, small_ref, a_ref, b_ref)


def space_second_kernel(
    scale_ref, u_ref, p_ref, recv_ref, dft_ref, small_ref, out_ref, r_ref, a_ref, b_ref
):
    for g in range(8):
        stack = jnp.concatenate([recv_ref[owner * 8 + g, 1] for owner in range(16)], axis=0).T
        for a in range(4):
            cols = slice(a * 128, a * 128 + 128)
            r_ref[g, :, cols] = p_ref[g, :, cols] + stack[a * 32 : a * 32 + 32]

    def get(m, lanes):
        g, cols = space_at(m, lanes)
        return (r_ref[g, 0:16, cols], r_ref[g, 16:32, cols])

    def put(m, lanes, values):
        g, cols = space_at(m, lanes)
        for half in range(2):
            rows = slice(16 * half, 16 * half + 16)
            out_ref[g, rows, cols] = values[0][half] - u_ref[g, rows, cols] * values[1][half]

    transform(get, put, 2, space_symbol(scale_ref[0], small_ref), dft_ref, small_ref, a_ref, b_ref)


def unturn_kernel(recv_ref, r_ref, gt_ref):
    for o, ref in enumerate((r_ref, gt_ref)):
        for h in range(2):
            for a in range(4):
                tile = recv_ref[:, o, 8 * a : 8 * a + 8, h * 128 : h * 128 + 128]
                ref[h * 128 : h * 128 + 128, a * 128 : a * 128 + 128] = tile.reshape(128, 128).T


def norm_kernel(gx_ref, gt_ref, cost_ref, out_ref):
    g = gx_ref[...] + gt_ref[...]
    norm = jnp.sum(g * g)
    cost = jnp.sum(cost_ref[...])
    lane = lax.broadcasted_iota(jnp.int32, (128, 128), 1)
    out_ref[...] = jnp.where(lane == 0, norm, cost)


def update_kernel(u_ref, gx_ref, gt_ref, sums_ref, out_ref):
    sums = jnp.sum(sums_ref[...], axis=0, keepdims=True)
    step = sums[:, 1:2] / (sums[:, 0:1] + GRAD_EPS)
    out_ref[...] = u_ref[...] - step * (gx_ref[...] + gt_ref[...])


VM = pl.BlockSpec(memory_space=pltpu.VMEM)
SM = pl.BlockSpec(memory_space=pltpu.SMEM)


def f32(*shape):
    return jax.ShapeDtypeStruct(shape, jnp.float32)


def call(kernel, outs, scalars, arrays, work=0, flops=0):
    scratch = []
    if work:
        scratch = [
            pltpu.VMEM((RADIX, 32, SUB), jnp.float32),
            pltpu.VMEM((work, RADIX, 32, SUB), jnp.float32),
        ]
    return pl.pallas_call(
        kernel,
        out_shape=outs,
        in_specs=[SM] * len(scalars) + [VM] * len(arrays),
        out_specs=jax.tree.map(lambda _: VM, outs),
        scratch_shapes=scratch,
        cost_estimate=pl.CostEstimate(flops=flops, bytes_accessed=2**21, transcendentals=0),
        compiler_params=pltpu.CompilerParams(vmem_limit_bytes=VMEM_LIMIT),
    )(*scalars, *arrays)


def local(field, time_period, space_period):
    dft_np, small_np = np_tables()
    dft = jnp.asarray(dft_np)
    small = jnp.asarray(small_np)
    time_scale = TWO_PI / time_period
    space_scale = TWO_PI / space_period
    every = ("ta", "gx")

    rows_u = lax.all_to_all(field.reshape(8, 32, 512), "gx", 0, 0)
    turned = call(turn_kernel, f32(16, 32, 256), [], [field])
    cols_u = lax.all_to_all(turned, "ta", 0, 0)

    p_pieces, rows_p = call(
        space_first_kernel,
        (f32(128, 8, 128), f32(8, 32, 512)),
        [space_scale],
        [rows_u, dft, small],
        work=2,
        flops=3 * 10**9,
    )
    q_pieces, cols_q = call(
        time_first_kernel,
        (f32(128, 8, 128), f32(16, 32, 256)),
        [time_scale],
        [cols_u, dft, small],
        work=1,
        flops=2 * 10**9,
    )
    pieces = jnp.stack([p_pieces, q_pieces], axis=1)
    received = lax.all_to_all(pieces, every, 0, 0)

    turned_back, cost = call(
        time_second_kernel,
        (f32(16, 2, 32, 256), f32(8, 128)),
        [time_scale],
        [cols_q, received, dft, small],
        work=1,
        flops=2 * 10**9,
    )
    back = lax.all_to_all(turned_back, "ta", 0, 0)
    rows_g, _ = call(
        space_second_kernel,
        (f32(8, 32, 512), f32(8, 32, 512)),
        [space_scale],
        [rows_u, rows_p, received, dft, small],
        work=2,
        flops=3 * 10**9,
    )
    gx = lax.all_to_all(rows_g, "gx", 0, 0).reshape(256, 512)
    residual, gt = call(unturn_kernel, (f32(256, 512), f32(256, 512)), [], [back])

    sums = call(norm_kernel, f32(128, 128), [], [gx, gt, cost])
    sums = lax.all_to_all(sums, every, 0, 0, tiled=True)
    updated = call(update_kernel, f32(256, 512), [], [field, gx, gt, sums])
    return updated, residual


def solution(mesh):
    placed = (P(("tile", "ta"), "gx"), P("tile"), P("tile"))
    return jax.shard_map(
        local,
        mesh=mesh,
        in_specs=placed,
        out_specs=(P(("tile", "ta"), "gx"), P(("tile", "ta"), "gx")),
        check_vma=False,
    )
```

```python
import math

import jax
import jax.numpy as jnp
import ml_dtypes
import numpy as np
from jax import lax
from jax.experimental import pallas as pl
from jax.experimental.pallas import tpu as pltpu
from jax.sharding import PartitionSpec as P

TWO_PI = 2.0 * math.pi
GRAD_EPS = 1e-06
LEN = 4096
RADIX = 16
SUB = 256
PARTS = 3
GROUP = 4
VMEM_LIMIT = 24 * 1024 * 1024


def np_parts(values):
    rest = np.asarray(values, np.float64)
    parts = []
    for _ in range(PARTS):
        part = rest.astype(np.float32).astype(ml_dtypes.bfloat16)
        parts.append(part)
        rest = rest - part.astype(np.float64)
    return parts


def np_tables():
    j = np.arange(SUB)
    angle = TWO_PI * (np.outer(j, j) % SUB) / SUB
    dft = np.stack(np_parts(np.cos(angle)) + np_parts(np.sin(angle)))
    k1 = np.arange(RADIX)
    twist = TWO_PI * np.outer(k1, j) / LEN
    mode = k1[:, None] + RADIX * j[None, :]
    signed = np.where(mode < LEN // 2, mode, mode - LEN)
    odd = np.where(mode == LEN // 2, 0, signed)
    small = np.stack([np.cos(twist), np.sin(twist), signed, odd]).astype(np.float32)
    return dft, small


def cadd(a, b):
    return (a[0] + b[0], a[1] + b[1])


def csub(a, b):
    return (a[0] - b[0], a[1] - b[1])


def dft4(x, sign):
    s = cadd(x[0], x[2])
    d = csub(x[0], x[2])
    t = cadd(x[1], x[3])
    e = csub(x[1], x[3])
    if sign < 0:
        ie = (e[1], -e[0])
    else:
        ie = (-e[1], e[0])
    return [cadd(s, t), cadd(d, ie), csub(s, t), csub(d, ie)]


def crot(x, turns, sign):
    if turns == 0:
        return x
    if turns == 4:
        return (x[1], -x[0]) if sign < 0 else (-x[1], x[0])
    c = math.cos(TWO_PI * turns / 16)
    s = sign * math.sin(TWO_PI * turns / 16)
    if turns == 2:
        return ((x[0] - sign * x[1]) * c, (x[1] + sign * x[0]) * c)
    if turns == 6:
        return ((x[0] + sign * x[1]) * c, (x[1] - sign * x[0]) * c)
    return (x[0] * c - x[1] * s, x[0] * s + x[1] * c)


def dft16(x, sign):
    out = [None] * 16
    rows = []
    for n2 in range(4):
        y = dft4([x[4 * n1 + n2] for n1 in range(4)], sign)
        rows.append([crot(y[k1], n2 * k1, sign) for k1 in range(4)])
    for k1 in range(4):
        z = dft4([rows[n2][k1] for n2 in range(4)], sign)
        for k2 in range(4):
            out[k1 + 4 * k2] = z[k2]
    return out


def split(values):
    parts = []
    rest = values
    for step in range(PARTS):
        part = rest.astype(jnp.bfloat16)
        parts.append(part)
        if step < PARTS - 1:
            rest = rest - part.astype(jnp.float32)
    return parts


def product(parts, table, first):
    total = None
    for order in reversed(range(PARTS)):
        for i in range(order + 1):
            term = jnp.dot(
                parts[i], table[first + order - i], preferred_element_type=jnp.float32
            )
            total = term if total is None else total + term
    return total


def transform(get, put, outputs, symbol, dft_ref, small_ref, a_ref, b_ref):
    for lane in range(2):
        lanes = slice(lane * 128, lane * 128 + 128)
        planes = dft16([get(m, lanes) for m in range(RADIX)], -1)
        for k1 in range(RADIX):
            re, im = planes[k1]
            if k1:
                c = small_ref[0, k1 : k1 + 1, lanes]
                s = small_ref[1, k1 : k1 + 1, lanes]
                re, im = re * c + im * s, im * c - re * s
            a_ref[k1, 0:16, lanes] = re
            a_ref[k1, 16:32, lanes] = im
    rows = GROUP * 16
    for group in range(RADIX // GROUP):
        ks = slice(group * GROUP, (group + 1) * GROUP)
        left = split(a_ref[ks].reshape(GROUP * 32, SUB))
        with_cos = product(left, dft_ref, 0).reshape(GROUP, 2, 16, SUB)
        with_sin = product(left, dft_ref, PARTS).reshape(GROUP, 2, 16, SUB)
        re = with_cos[:, 0] + with_sin[:, 1]
        im = with_cos[:, 1] - with_sin[:, 0]
        for o in range(outputs):
            sre, sim = symbol(o, ks, re, im)
            left = split(jnp.concatenate([sre, sim], axis=1).reshape(GROUP * 32, SUB))
            with_cos = product(left, dft_ref, 0).reshape(GROUP, 2, 16, SUB)
            with_sin = product(left, dft_ref, PARTS).reshape(GROUP, 2, 16, SUB)
            re2 = with_cos[:, 0] - with_sin[:, 1]
            im2 = with_cos[:, 1] + with_sin[:, 0]
            c = small_ref[0, ks][:, None, :]
            s = small_ref[1, ks][:, None, :]
            b_ref[o, ks, 0:16] = re2 * c - im2 * s
            b_ref[o, ks, 16:32] = im2 * c + re2 * s
    for lane in range(2):
        lanes = slice(lane * 128, lane * 128 + 128)
        outs = []
        for o in range(outputs):
            planes = [(b_ref[o, k, 0:16, lanes], b_ref[o, k, 16:32, lanes]) for k in range(RADIX)]
            outs.append(dft16(planes, 1))
        for m in range(RADIX):
            put(m, lanes, [outs[o][m] for o in range(outputs)])


def space_symbol(scale, small_ref):
    def symbol(o, ks, re, im):
        if o == 0:
            wave = small_ref[2, ks] * scale
            square = wave * wave
            even = ((square * square - square) * (1.0 / LEN))[:, None, :]
            return re * even, im * even
        odd = (small_ref[3, ks] * (scale * (1.0 / LEN)))[:, None, :]
        return -im * odd, re * odd

    return symbol


def time_symbol(scale, small_ref):
    def symbol(o, ks, re, im):
        odd = (small_ref[3, ks] * (scale * (1.0 / LEN)))[:, None, :]
        return -im * odd, re * odd

    return symbol


def space_at(m, lanes):
    start = (m % 2) * 256 + lanes.start
    return m // 2, slice(start, start + 128)


def blocks4(tiles):
    lane = lax.broadcasted_iota(jnp.int32, tiles[0].shape, len(tiles[0].shape) - 1)
    axis = len(tiles[0].shape) - 1
    low_half = lane < 64
    even = (lane // 32) % 2 == 0

    def swap(x, y, shift, mask):
        first = jnp.where(mask, x, pltpu.roll(y, shift, axis))
        second = jnp.where(mask, pltpu.roll(x, 128 - shift, axis), y)
        return first, second

    t0, t2 = swap(tiles[0], tiles[2], 64, low_half)
    t1, t3 = swap(tiles[1], tiles[3], 64, low_half)
    t0, t1 = swap(t0, t1, 32, even)
    t2, t3 = swap(t2, t3, 32, even)
    return [t0, t1, t2, t3]


def turn_kernel(u_ref, out_ref):
    for h in range(2):
        for a in range(4):
            tile = u_ref[h * 128 : h * 128 + 128, a * 128 : a * 128 + 128].T
            out_ref[:, a * 8 : a * 8 + 8, h * 128 : h * 128 + 128] = tile.reshape(16, 8, 128)


def space_kernel(scale_ref, u_ref, dft_ref, small_ref, out_ref, p_ref, v_ref, a_ref, b_ref):
    def send(slot, ref):
        for g in range(8):
            stack = jnp.concatenate([ref[g, :, a * 128 : a * 128 + 128] for a in range(4)], axis=0)
            turned = stack.T.reshape(16, 8, 128)
            for owner in range(16):
                out_ref[owner * 8 + g, 8 * slot : 8 * slot + 8] = turned[owner]

    def get_u(m, lanes):
        g, cols = space_at(m, lanes)
        return (u_ref[g, 0:16, cols], u_ref[g, 16:32, cols])

    def put_u(m, lanes, values):
        g, cols = space_at(m, lanes)
        for half in range(2):
            rows = slice(16 * half, 16 * half + 16)
            p_ref[g, rows, cols] = values[0][half] + u_ref[g, rows, cols] * values[1][half]
            v_ref[g, rows, cols] = values[1][half]

    def get_p(m, lanes):
        g, cols = space_at(m, lanes)
        return (p_ref[g, 0:16, cols], p_ref[g, 16:32, cols])

    def put_p(m, lanes, values):
        g, cols = space_at(m, lanes)
        for half in range(2):
            rows = slice(16 * half, 16 * half + 16)
            v_ref[g, rows, cols] = values[0][half] - u_ref[g, rows, cols] * values[1][half]

    symbol = space_symbol(scale_ref[0], small_ref)
    transform(get_u, put_u, 2, symbol, dft_ref, small_ref, a_ref, b_ref)
    send(0, v_ref)
    send(1, p_ref)
    transform(get_p, put_p, 2, symbol, dft_ref, small_ref, a_ref, b_ref)
    send(2, v_ref)


def time_first_kernel(scale_ref, u_ref, dft_ref, small_ref, q_ref, a_ref, b_ref):
    def get(m, lanes):
        return (u_ref[m, 0:16, lanes], u_ref[m, 16:32, lanes])

    def put(m, lanes, values):
        q_ref[m, 0:16, lanes] = values[0][0]
        q_ref[m, 16:32, lanes] = values[0][1]

    transform(get, put, 1, time_symbol(scale_ref[0], small_ref), dft_ref, small_ref, a_ref, b_ref)


def time_second_kernel(
    scale_ref, u_ref, q_ref, recv_ref, dft_ref, small_ref, out_ref, v_ref, s_ref, g_ref, a_ref, b_ref
):
    cost = jnp.zeros((8, 128), jnp.float32)
    for m in range(16):
        for h in range(2):
            cols = slice(h * 128, h * 128 + 128)
            tiles = [
                blocks4([recv_ref[m * 8 + 4 * h + k, 8 * o : 8 * o + 8] for k in range(4)])
                for o in range(3)
            ]
            for a in range(4):
                rows = slice(8 * a, 8 * a + 8)
                q = q_ref[m, rows, cols]
                v_ref[m, rows, cols] = tiles[0][a]
                s_ref[m, rows, cols] = q + u_ref[m, rows, cols] * tiles[0][a]
                r = q + tiles[1][a]
                out_ref[m, rows, cols] = r
                cost = cost + r * r
                g_ref[m, rows, cols] = tiles[2][a]

    halves = (slice(0, 16), slice(16, 32))
    norm = [jnp.zeros((16, 128), jnp.float32)]

    def get_v(m, lanes):
        return tuple(v_ref[m, rows, lanes] for rows in halves)

    def put_v(m, lanes, values):
        for half, rows in enumerate(halves):
            g_ref[m, rows, lanes] = (
                g_ref[m, rows, lanes] - u_ref[m, rows, lanes] * values[0][half]
            )

    def get_s(m, lanes):
        return tuple(s_ref[m, rows, lanes] for rows in halves)

    def put_s(m, lanes, values):
        for half, rows in enumerate(halves):
            g = g_ref[m, rows, lanes] - values[0][half]
            out_ref[m, 32 + rows.start : 32 + rows.stop, lanes] = g
            norm[0] = norm[0] + g * g

    symbol = time_symbol(scale_ref[0], small_ref)
    transform(get_v, put_v, 1, symbol, dft_ref, small_ref, a_ref, b_ref)
    transform(get_s, put_s, 1, symbol, dft_ref, small_ref, a_ref, b_ref)
    norm = norm[0][0:8] + norm[0][8:16]
    for m in range(16):
        out_ref[m, 64:72, 0:128] = 0.5 * cost
        out_ref[m, 64:72, 128:256] = norm


def sums_kernel(recv_ref, out_ref):
    total = jnp.sum(recv_ref[:, 64:72, :], axis=0)
    cost = jnp.sum(total[:, 0:128], axis=0, keepdims=True)
    norm = jnp.sum(total[:, 128:256], axis=0, keepdims=True)
    row = lax.broadcasted_iota(jnp.int32, (8, 128), 0)
    out_ref[...] = jnp.broadcast_to(jnp.where(row == 0, cost, norm)[None], (8, 8, 128))


def unturn_kernel(recv_ref, r_ref, g_ref):
    for o, ref in enumerate((r_ref, g_ref)):
        for h in range(2):
            for a in range(4):
                first = 32 * o + 8 * a
                tile = recv_ref[:, first : first + 8, h * 128 : h * 128 + 128]
                ref[h * 128 : h * 128 + 128, a * 128 : a * 128 + 128] = tile.reshape(128, 128).T


def update_kernel(u_ref, g_ref, sums_ref, out_ref):
    sums = jnp.sum(sums_ref[...], axis=0)
    cost = jnp.sum(sums[0:1, :], axis=1, keepdims=True)
    norm = jnp.sum(sums[1:2, :], axis=1, keepdims=True)
    out_ref[...] = u_ref[...] - (cost / (norm + GRAD_EPS)) * g_ref[...]


VM = pl.BlockSpec(memory_space=pltpu.VMEM)
SM = pl.BlockSpec(memory_space=pltpu.SMEM)


def f32(*shape):
    return jax.ShapeDtypeStruct(shape, jnp.float32)


def call(kernel, outs, scalars, arrays, scratch=(), flops=0):
    return pl.pallas_call(
        kernel,
        out_shape=outs,
        in_specs=[SM] * len(scalars) + [VM] * len(arrays),
        out_specs=jax.tree.map(lambda _: VM, outs),
        scratch_shapes=[pltpu.VMEM(shape, jnp.float32) for shape in scratch],
        cost_estimate=pl.CostEstimate(flops=flops, bytes_accessed=2**21, transcendentals=0),
        compiler_params=pltpu.CompilerParams(vmem_limit_bytes=VMEM_LIMIT),
    )(*scalars, *arrays)


def local(field, time_period, space_period):
    dft_np, small_np = np_tables()
    dft = jnp.asarray(dft_np)
    small = jnp.asarray(small_np)
    time_scale = TWO_PI / time_period
    space_scale = TWO_PI / space_period
    every = ("ta", "gx")
    rows, cols = (8, 32, 512), (16, 32, 256)
    planes = (RADIX, 32, SUB)

    rows_u = lax.all_to_all(field.reshape(rows), "gx", 0, 0)
    turned = call(turn_kernel, f32(*cols), [], [field])
    rows_u, turned = lax.optimization_barrier((rows_u, turned))
    cols_u = lax.all_to_all(turned, "ta", 0, 0)

    pieces = call(
        space_kernel,
        f32(128, 24, 128),
        [space_scale],
        [rows_u, dft, small],
        [rows, rows, planes, (2, *planes)],
        flops=8 * 10**9,
    )
    received = lax.all_to_all(pieces, every, 0, 0)
    cols_q = call(
        time_first_kernel,
        f32(*cols),
        [time_scale],
        [cols_u, dft, small],
        [planes, (1, *planes)],
        flops=2 * 10**9,
    )
    cols_out = call(
        time_second_kernel,
        f32(16, 72, 256),
        [time_scale],
        [cols_u, cols_q, received, dft, small],
        [cols, cols, cols, planes, (1, *planes)],
        flops=4 * 10**9,
    )
    back = lax.all_to_all(cols_out, "ta", 0, 0)
    sums = call(sums_kernel, f32(8, 8, 128), [], [back])
    sums = lax.all_to_all(sums, "gx", 0, 0)
    residual, gradient = call(unturn_kernel, (f32(256, 512), f32(256, 512)), [], [back])
    updated = call(update_kernel, f32(256, 512), [], [field, gradient, sums])
    return updated, residual


def solution(mesh):
    placed = (P(("tile", "ta"), "gx"), P("tile"), P("tile"))
    return jax.shard_map(
        local,
        mesh=mesh,
        in_specs=placed,
        out_specs=(P(("tile", "ta"), "gx"), P(("tile", "ta"), "gx")),
        check_vma=False,
    )
```

```python
import math

import jax
import jax.numpy as jnp
import ml_dtypes
import numpy as np
from jax import lax
from jax.experimental import pallas as pl
from jax.experimental.pallas import tpu as pltpu
from jax.sharding import PartitionSpec as P

TWO_PI = 2.0 * math.pi
GRAD_EPS = 1e-06
LEN = 4096
RADIX = 32
SUB = 128
PARTS = 3
GROUP = 8
VMEM_LIMIT = 24 * 1024 * 1024


def np_parts(values):
    rest = np.asarray(values, np.float64)
    parts = []
    for _ in range(PARTS):
        part = rest.astype(np.float32).astype(ml_dtypes.bfloat16)
        parts.append(part)
        rest = rest - part.astype(np.float64)
    return parts


def np_tables():
    j = np.arange(SUB)
    angle = TWO_PI * (np.outer(j, j) % SUB) / SUB
    cos, sin = np.cos(angle), np.sin(angle)
    dft = np.stack(np_parts(np.block([[cos, -sin], [sin, cos]])))
    k1 = np.arange(RADIX)
    twist = TWO_PI * np.outer(k1, j) / LEN
    mode = k1[:, None] + RADIX * j[None, :]
    signed = np.where(mode < LEN // 2, mode, mode - LEN)
    odd = np.where(mode == LEN // 2, 0, signed)
    small = np.stack([np.cos(twist), np.sin(twist), signed, odd]).astype(np.float32)
    return dft, small


def cadd(a, b):
    return (a[0] + b[0], a[1] + b[1])


def csub(a, b):
    return (a[0] - b[0], a[1] - b[1])


def dft4(x, sign):
    s = cadd(x[0], x[2])
    d = csub(x[0], x[2])
    t = cadd(x[1], x[3])
    e = csub(x[1], x[3])
    if sign < 0:
        ie = (e[1], -e[0])
    else:
        ie = (-e[1], e[0])
    return [cadd(s, t), cadd(d, ie), csub(s, t), csub(d, ie)]


def crot(x, turns, sign):
    turns = turns % 32
    if turns == 0:
        return x
    if turns == 8:
        return (x[1], -x[0]) if sign < 0 else (-x[1], x[0])
    c = math.cos(TWO_PI * turns / 32)
    s = sign * math.sin(TWO_PI * turns / 32)
    if turns == 4:
        return ((x[0] - sign * x[1]) * c, (x[1] + sign * x[0]) * c)
    if turns == 12:
        return ((x[0] + sign * x[1]) * c, (x[1] - sign * x[0]) * c)
    return (x[0] * c - x[1] * s, x[0] * s + x[1] * c)


def dft8(x, sign):
    even = dft4(x[0::2], sign)
    odd = [crot(value, 4 * k, sign) for k, value in enumerate(dft4(x[1::2], sign))]
    return [cadd(even[k], odd[k]) for k in range(4)] + [csub(even[k], odd[k]) for k in range(4)]


def dft32(x, sign):
    out = [None] * 32
    rows = []
    for n2 in range(8):
        y = dft4([x(8 * n1 + n2) for n1 in range(4)], sign)
        rows.append([crot(y[k1], n2 * k1, sign) for k1 in range(4)])
    for k1 in range(4):
        z = dft8([rows[n2][k1] for n2 in range(8)], sign)
        for k2 in range(8):
            out[k1 + 4 * k2] = z[k2]
    return out


def product(values, table_ref):
    parts = []
    rest = values
    for step in range(PARTS):
        part = rest.astype(jnp.bfloat16)
        parts.append(part)
        if step < PARTS - 1:
            rest = rest - part.astype(jnp.float32)
    order = [(i, k - i) for k in reversed(range(PARTS)) for i in range(k + 1)]
    left = jnp.concatenate([parts[i] for i, _ in order], axis=1)
    right = jnp.concatenate([table_ref[j] for _, j in order], axis=0)
    return jnp.dot(left, right, preferred_element_type=jnp.float32)


def transform(get, put, outputs, symbol, dft_ref, small_ref, a_ref, b_ref):
    re_lanes, im_lanes = slice(0, SUB), slice(SUB, 2 * SUB)
    for half in range(2):
        rows = slice(8 * half, 8 * half + 8)
        planes = dft32(lambda m: get(m, half), -1)
        for k1 in range(RADIX):
            re, im = planes[k1]
            if k1:
                c = small_ref[0, k1 : k1 + 1, :]
                s = small_ref[1, k1 : k1 + 1, :]
                re, im = re * c + im * s, im * c - re * s
            a_ref[k1, rows, re_lanes] = re
            a_ref[k1, rows, im_lanes] = im
    for group in range(RADIX // GROUP):
        ks = slice(group * GROUP, (group + 1) * GROUP)
        got = product(a_ref[ks].reshape(GROUP * 16, 2 * SUB), dft_ref)
        got = got.reshape(GROUP, 16, 2 * SUB)
        re, im = got[:, :, re_lanes], got[:, :, im_lanes]
        for o in range(outputs):
            swapped = jnp.concatenate(symbol(o, ks, re, im)[::-1], axis=2)
            got = product(swapped.reshape(GROUP * 16, 2 * SUB), dft_ref)
            got = got.reshape(GROUP, 16, 2 * SUB)
            im2, re2 = got[:, :, re_lanes], got[:, :, im_lanes]
            c = small_ref[0, ks][:, None, :]
            s = small_ref[1, ks][:, None, :]
            b_ref[o, ks, :, re_lanes] = re2 * c - im2 * s
            b_ref[o, ks, :, im_lanes] = im2 * c + re2 * s
    for half in range(2):
        rows = slice(8 * half, 8 * half + 8)
        outs = [
            dft32(lambda k: (b_ref[o, k, rows, re_lanes], b_ref[o, k, rows, im_lanes]), 1)
            for o in range(outputs)
        ]
        for m in range(RADIX):
            put(m, half, [outs[o][m] for o in range(outputs)])


def space_symbol(scale, small_ref):
    def symbol(o, ks, re, im):
        if o == 0:
            wave = small_ref[2, ks] * scale
            square = wave * wave
            even = ((square * square - square) * (1.0 / LEN))[:, None, :]
            return re * even, im * even
        odd = (small_ref[3, ks] * (scale * (1.0 / LEN)))[:, None, :]
        return -im * odd, re * odd

    return symbol


def time_symbol(scale, small_ref):
    def symbol(o, ks, re, im):
        odd = (small_ref[3, ks] * (scale * (1.0 / LEN)))[:, None, :]
        return -im * odd, re * odd

    return symbol


def row_parts(half):
    return slice(8 * half, 8 * half + 8), slice(16 + 8 * half, 24 + 8 * half)


def space_at(m):
    return m // 4, slice((m % 4) * 128, (m % 4) * 128 + 128)


def time_at(m):
    return m // 2, slice((m % 2) * 128, (m % 2) * 128 + 128)


def blocks4(tiles):
    lane = lax.broadcasted_iota(jnp.int32, tiles[0].shape, len(tiles[0].shape) - 1)
    axis = len(tiles[0].shape) - 1
    low_half = lane < 64
    even = (lane // 32) % 2 == 0

    def swap(x, y, shift, mask):
        first = jnp.where(mask, x, pltpu.roll(y, shift, axis))
        second = jnp.where(mask, pltpu.roll(x, 128 - shift, axis), y)
        return first, second

    t0, t2 = swap(tiles[0], tiles[2], 64, low_half)
    t1, t3 = swap(tiles[1], tiles[3], 64, low_half)
    t0, t1 = swap(t0, t1, 32, even)
    t2, t3 = swap(t2, t3, 32, even)
    return [t0, t1, t2, t3]


def turn_kernel(u_ref, out_ref):
    for h in range(2):
        for a in range(4):
            tile = u_ref[h * 128 : h * 128 + 128, a * 128 : a * 128 + 128].T
            out_ref[:, a * 8 : a * 8 + 8, h * 128 : h * 128 + 128] = tile.reshape(16, 8, 128)


def space_kernel(scale_ref, u_ref, dft_ref, small_ref, out_ref, p_ref, v_ref, a_ref, b_ref):
    def send(slot, ref):
        for g in range(8):
            stack = jnp.concatenate([ref[g, :, a * 128 : a * 128 + 128] for a in range(4)], axis=0)
            turned = stack.T.reshape(16, 8, 128)
            for owner in range(16):
                out_ref[owner * 8 + g, 8 * slot : 8 * slot + 8] = turned[owner]

    def get_u(m, half):
        g, cols = space_at(m)
        return tuple(u_ref[g, rows, cols] for rows in row_parts(half))

    def put_u(m, half, values):
        g, cols = space_at(m)
        for part, rows in enumerate(row_parts(half)):
            p_ref[g, rows, cols] = values[0][part] + u_ref[g, rows, cols] * values[1][part]
            v_ref[g, rows, cols] = values[1][part]

    def get_p(m, half):
        g, cols = space_at(m)
        return tuple(p_ref[g, rows, cols] for rows in row_parts(half))

    def put_p(m, half, values):
        g, cols = space_at(m)
        for part, rows in enumerate(row_parts(half)):
            v_ref[g, rows, cols] = values[0][part] - u_ref[g, rows, cols] * values[1][part]

    symbol = space_symbol(scale_ref[0], small_ref)
    transform(get_u, put_u, 2, symbol, dft_ref, small_ref, a_ref, b_ref)
    send(0, v_ref)
    send(1, p_ref)
    transform(get_p, put_p, 2, symbol, dft_ref, small_ref, a_ref, b_ref)
    send(2, v_ref)


def time_first_kernel(
    scale_ref, place_ref, moved_ref, dft_ref, small_ref, u_ref, q_ref, a_ref, b_ref
):
    for m in range(16):
        u_ref[m] = moved_ref[(place_ref[0] + 4 - m // 4) % 4, (place_ref[1] + 4 - m % 4) % 4]

    def get(m, half):
        t, cols = time_at(m)
        return tuple(u_ref[t, rows, cols] for rows in row_parts(half))

    def put(m, half, values):
        t, cols = time_at(m)
        for part, rows in enumerate(row_parts(half)):
            q_ref[t, rows, cols] = values[0][part]

    transform(get, put, 1, time_symbol(scale_ref[0], small_ref), dft_ref, small_ref, a_ref, b_ref)


def time_second_kernel(
    scale_ref, u_ref, q_ref, recv_ref, dft_ref, small_ref, out_ref, v_ref, s_ref, g_ref, a_ref, b_ref
):
    cost = jnp.zeros((8, 128), jnp.float32)
    for m in range(16):
        for h in range(2):
            cols = slice(h * 128, h * 128 + 128)
            tiles = [
                blocks4([recv_ref[m * 8 + 4 * h + k, 8 * o : 8 * o + 8] for k in range(4)])
                for o in range(3)
            ]
            for a in range(4):
                rows = slice(8 * a, 8 * a + 8)
                q = q_ref[m, rows, cols]
                v_ref[m, rows, cols] = tiles[0][a]
                s_ref[m, rows, cols] = q + u_ref[m, rows, cols] * tiles[0][a]
                r = q + tiles[1][a]
                out_ref[m, rows, cols] = r
                cost = cost + r * r
                g_ref[m, rows, cols] = tiles[2][a]

    norm = [jnp.zeros((8, 128), jnp.float32)]

    def get_v(m, half):
        t, cols = time_at(m)
        return tuple(v_ref[t, rows, cols] for rows in row_parts(half))

    def put_v(m, half, values):
        t, cols = time_at(m)
        for part, rows in enumerate(row_parts(half)):
            g_ref[t, rows, cols] = g_ref[t, rows, cols] - u_ref[t, rows, cols] * values[0][part]

    def get_s(m, half):
        t, cols = time_at(m)
        return tuple(s_ref[t, rows, cols] for rows in row_parts(half))

    def put_s(m, half, values):
        t, cols = time_at(m)
        for part, rows in enumerate(row_parts(half)):
            g = g_ref[t, rows, cols] - values[0][part]
            out_ref[t, 32 + rows.start : 32 + rows.stop, cols] = g
            norm[0] = norm[0] + g * g

    symbol = time_symbol(scale_ref[0], small_ref)
    transform(get_v, put_v, 1, symbol, dft_ref, small_ref, a_ref, b_ref)
    transform(get_s, put_s, 1, symbol, dft_ref, small_ref, a_ref, b_ref)
    for m in range(16):
        out_ref[m, 64:72, 0:128] = 0.5 * cost
        out_ref[m, 64:72, 128:256] = norm[0]


def sums_kernel(recv_ref, out_ref):
    total = jnp.sum(recv_ref[:, 64:72, :], axis=0)
    cost = jnp.sum(total[:, 0:128], axis=0, keepdims=True)
    norm = jnp.sum(total[:, 128:256], axis=0, keepdims=True)
    row = lax.broadcasted_iota(jnp.int32, (8, 128), 0)
    out_ref[...] = jnp.broadcast_to(jnp.where(row == 0, cost, norm)[None], (8, 8, 128))


def unturn_kernel(recv_ref, r_ref, g_ref):
    for o, ref in enumerate((r_ref, g_ref)):
        for h in range(2):
            for a in range(4):
                first = 32 * o + 8 * a
                tile = recv_ref[:, first : first + 8, h * 128 : h * 128 + 128]
                ref[h * 128 : h * 128 + 128, a * 128 : a * 128 + 128] = tile.reshape(128, 128).T


def update_kernel(u_ref, g_ref, sums_ref, out_ref):
    sums = jnp.sum(sums_ref[...], axis=0)
    cost = jnp.sum(sums[0:1, :], axis=1, keepdims=True)
    norm = jnp.sum(sums[1:2, :], axis=1, keepdims=True)
    out_ref[...] = u_ref[...] - (cost / (norm + GRAD_EPS)) * g_ref[...]


VM = pl.BlockSpec(memory_space=pltpu.VMEM)
SM = pl.BlockSpec(memory_space=pltpu.SMEM)


def f32(*shape):
    return jax.ShapeDtypeStruct(shape, jnp.float32)


def call(kernel, outs, scalars, arrays, scratch=(), flops=0):
    return pl.pallas_call(
        kernel,
        out_shape=outs,
        in_specs=[SM] * len(scalars) + [VM] * len(arrays),
        out_specs=jax.tree.map(lambda _: VM, outs),
        scratch_shapes=[pltpu.VMEM(shape, jnp.float32) for shape in scratch],
        cost_estimate=pl.CostEstimate(flops=flops, bytes_accessed=2**21, transcendentals=0),
        compiler_params=pltpu.CompilerParams(vmem_limit_bytes=VMEM_LIMIT),
    )(*scalars, *arrays)


def shift_pairs(axis, shift):
    pairs = []
    for y in range(4):
        for x in range(4):
            to = (y, (x + shift) % 4) if axis else ((y + shift) % 4, x)
            pairs.append((4 * y + x, 4 * to[0] + to[1]))
    return pairs


def to_columns(turned):
    here = lax.axis_index("ta")
    y, x = here // 4, here % 4
    pieces = turned.reshape(4, 4, 32, 256)
    along_x = []
    for d in range(4):
        piece = lax.dynamic_index_in_dim(pieces, (x + d) % 4, 1, keepdims=False)
        along_x.append(lax.ppermute(piece, "ta", shift_pairs(1, d)) if d else piece)
    along_y = []
    for e in range(4):
        piece = jnp.stack(
            [lax.dynamic_index_in_dim(part, (y + e) % 4, 0, keepdims=False) for part in along_x]
        )
        along_y.append(lax.ppermute(piece, "ta", shift_pairs(0, e)) if e else piece)
    return jnp.stack(along_y), jnp.stack([y, x])


def local(field, time_period, space_period):
    dft_np, small_np = np_tables()
    dft = jnp.asarray(dft_np)
    small = jnp.asarray(small_np)
    time_scale = TWO_PI / time_period
    space_scale = TWO_PI / space_period
    every = ("ta", "gx")
    rows, cols = (8, 32, 512), (16, 32, 256)
    planes = (RADIX, 16, 2 * SUB)

    rows_u = lax.all_to_all(field.reshape(rows), "gx", 0, 0)
    turned = call(turn_kernel, f32(*cols), [], [field])
    pieces = call(
        space_kernel,
        f32(128, 24, 128),
        [space_scale],
        [rows_u, dft, small],
        [rows, rows, planes, (2, *planes)],
        flops=8 * 10**9,
    )
    pieces, turned = lax.optimization_barrier((pieces, turned))
    received = lax.all_to_all(pieces, every, 0, 0)
    moved, place = to_columns(turned)
    cols_u, cols_q = call(
        time_first_kernel,
        (f32(*cols), f32(*cols)),
        [time_scale, place],
        [moved, dft, small],
        [planes, (1, *planes)],
        flops=2 * 10**9,
    )
    cols_out = call(
        time_second_kernel,
        f32(16, 72, 256),
        [time_scale],
        [cols_u, cols_q, received, dft, small],
        [cols, cols, cols, planes, (1, *planes)],
        flops=4 * 10**9,
    )
    back = lax.all_to_all(cols_out, "ta", 0, 0)
    sums = call(sums_kernel, f32(8, 8, 128), [], [back])
    sums = lax.all_to_all(sums, "gx", 0, 0)
    residual, gradient = call(unturn_kernel, (f32(256, 512), f32(256, 512)), [], [back])
    updated = call(update_kernel, f32(256, 512), [], [field, gradient, sums])
    return updated, residual


def solution(mesh):
    placed = (P(("tile", "ta"), "gx"), P("tile"), P("tile"))
    return jax.shard_map(
        local,
        mesh=mesh,
        in_specs=placed,
        out_specs=(P(("tile", "ta"), "gx"), P(("tile", "ta"), "gx")),
        check_vma=False,
    )
```

```python
import math

import jax
import jax.numpy as jnp
import ml_dtypes
import numpy as np
from jax import lax
from jax.experimental import pallas as pl
from jax.experimental.pallas import tpu as pltpu
from jax.sharding import PartitionSpec as P

TWO_PI = 2.0 * math.pi
GRAD_EPS = 1e-06
LEN = 4096
RADIX = 32
SUB = 128
PARTS = 3
GROUP = 8
VMEM_LIMIT = 24 * 1024 * 1024


def np_parts(values):
    rest = np.asarray(values, np.float64)
    parts = []
    for _ in range(PARTS):
        part = rest.astype(np.float32).astype(ml_dtypes.bfloat16)
        parts.append(part)
        rest = rest - part.astype(np.float64)
    return parts


def np_tables():
    j = np.arange(SUB)
    angle = TWO_PI * (np.outer(j, j) % SUB) / SUB
    cos, sin = np.cos(angle), np.sin(angle)
    dft = np.stack(np_parts(np.block([[cos, -sin], [sin, cos]])))
    k1 = np.arange(RADIX)
    twist = TWO_PI * np.outer(k1, j) / LEN
    mode = k1[:, None] + RADIX * j[None, :]
    signed = np.where(mode < LEN // 2, mode, mode - LEN)
    odd = np.where(mode == LEN // 2, 0, signed)
    small = np.stack([np.cos(twist), np.sin(twist), signed, odd]).astype(np.float32)
    return dft, small


def cadd(a, b):
    return (a[0] + b[0], a[1] + b[1])


def csub(a, b):
    return (a[0] - b[0], a[1] - b[1])


def dft4(x, sign):
    s = cadd(x[0], x[2])
    d = csub(x[0], x[2])
    t = cadd(x[1], x[3])
    e = csub(x[1], x[3])
    if sign < 0:
        ie = (e[1], -e[0])
    else:
        ie = (-e[1], e[0])
    return [cadd(s, t), cadd(d, ie), csub(s, t), csub(d, ie)]


def crot(x, turns, sign):
    turns = turns % 32
    if turns == 0:
        return x
    if turns == 8:
        return (x[1], -x[0]) if sign < 0 else (-x[1], x[0])
    c = math.cos(TWO_PI * turns / 32)
    s = sign * math.sin(TWO_PI * turns / 32)
    if turns == 4:
        return ((x[0] - sign * x[1]) * c, (x[1] + sign * x[0]) * c)
    if turns == 12:
        return ((x[0] + sign * x[1]) * c, (x[1] - sign * x[0]) * c)
    return (x[0] * c - x[1] * s, x[0] * s + x[1] * c)


def dft8(x, sign):
    even = dft4(x[0::2], sign)
    odd = [crot(value, 4 * k, sign) for k, value in enumerate(dft4(x[1::2], sign))]
    return [cadd(even[k], odd[k]) for k in range(4)] + [csub(even[k], odd[k]) for k in range(4)]


def dft32(x, sign):
    out = [None] * 32
    rows = []
    for n2 in range(8):
        y = dft4([x(8 * n1 + n2) for n1 in range(4)], sign)
        rows.append([crot(y[k1], n2 * k1, sign) for k1 in range(4)])
    for k1 in range(4):
        z = dft8([rows[n2][k1] for n2 in range(8)], sign)
        for k2 in range(8):
            out[k1 + 4 * k2] = z[k2]
    return out


def product(values, table_ref):
    parts = []
    rest = values
    for step in range(PARTS):
        part = rest.astype(jnp.bfloat16)
        parts.append(part)
        if step < PARTS - 1:
            rest = rest - part.astype(jnp.float32)
    order = [(i, k - i) for k in reversed(range(PARTS)) for i in range(k + 1)]
    left = jnp.concatenate([parts[i] for i, _ in order], axis=1)
    right = jnp.concatenate([table_ref[j] for _, j in order], axis=0)
    return jnp.dot(left, right, preferred_element_type=jnp.float32)


def transform(get, put, outputs, symbol, dft_ref, small_ref, a_ref, b_ref):
    re_lanes, im_lanes = slice(0, SUB), slice(SUB, 2 * SUB)
    for half in range(2):
        rows = slice(8 * half, 8 * half + 8)
        planes = dft32(lambda m: get(m, half), -1)
        for k1 in range(RADIX):
            re, im = planes[k1]
            if k1:
                c = small_ref[0, k1 : k1 + 1, :]
                s = small_ref[1, k1 : k1 + 1, :]
                re, im = re * c + im * s, im * c - re * s
            a_ref[k1, rows, re_lanes] = re
            a_ref[k1, rows, im_lanes] = im
    for group in range(RADIX // GROUP):
        ks = slice(group * GROUP, (group + 1) * GROUP)
        got = product(a_ref[ks].reshape(GROUP * 16, 2 * SUB), dft_ref)
        got = got.reshape(GROUP, 16, 2 * SUB)
        re, im = got[:, :, re_lanes], got[:, :, im_lanes]
        for o in range(outputs):
            swapped = jnp.concatenate(symbol(o, ks, re, im)[::-1], axis=2)
            got = product(swapped.reshape(GROUP * 16, 2 * SUB), dft_ref)
            got = got.reshape(GROUP, 16, 2 * SUB)
            im2, re2 = got[:, :, re_lanes], got[:, :, im_lanes]
            c = small_ref[0, ks][:, None, :]
            s = small_ref[1, ks][:, None, :]
            b_ref[o, ks, :, re_lanes] = re2 * c - im2 * s
            b_ref[o, ks, :, im_lanes] = im2 * c + re2 * s
    for half in range(2):
        rows = slice(8 * half, 8 * half + 8)
        outs = [
            dft32(lambda k: (b_ref[o, k, rows, re_lanes], b_ref[o, k, rows, im_lanes]), 1)
            for o in range(outputs)
        ]
        for m in range(RADIX):
            put(m, half, [outs[o][m] for o in range(outputs)])


def space_symbol(scale, small_ref):
    def symbol(o, ks, re, im):
        if o == 0:
            wave = small_ref[2, ks] * scale
            square = wave * wave
            even = ((square * square - square) * (1.0 / LEN))[:, None, :]
            return re * even, im * even
        odd = (small_ref[3, ks] * (scale * (1.0 / LEN)))[:, None, :]
        return -im * odd, re * odd

    return symbol


def time_symbol(scale, small_ref):
    def symbol(o, ks, re, im):
        odd = (small_ref[3, ks] * (scale * (1.0 / LEN)))[:, None, :]
        return -im * odd, re * odd

    return symbol


def row_parts(half):
    return slice(8 * half, 8 * half + 8), slice(16 + 8 * half, 24 + 8 * half)


def space_at(m):
    return m // 4, slice((m % 4) * 128, (m % 4) * 128 + 128)


def time_at(m):
    return m // 2, slice((m % 2) * 128, (m % 2) * 128 + 128)


def blocks4(tiles):
    lane = lax.broadcasted_iota(jnp.int32, tiles[0].shape, len(tiles[0].shape) - 1)
    axis = len(tiles[0].shape) - 1
    low_half = lane < 64
    even = (lane // 32) % 2 == 0

    def swap(x, y, shift, mask):
        first = jnp.where(mask, x, pltpu.roll(y, shift, axis))
        second = jnp.where(mask, pltpu.roll(x, 128 - shift, axis), y)
        return first, second

    t0, t2 = swap(tiles[0], tiles[2], 64, low_half)
    t1, t3 = swap(tiles[1], tiles[3], 64, low_half)
    t0, t1 = swap(t0, t1, 32, even)
    t2, t3 = swap(t2, t3, 32, even)
    return [t0, t1, t2, t3]


def turn_kernel(u_ref, out_ref):
    for h in range(2):
        for a in range(4):
            tile = u_ref[h * 128 : h * 128 + 128, a * 128 : a * 128 + 128].T
            out_ref[:, a * 8 : a * 8 + 8, h * 128 : h * 128 + 128] = tile.reshape(16, 8, 128)


def space_kernel(
    scale_ref,
    place_ref,
    u_ref,
    dft_ref,
    small_ref,
    out_ref,
    *rest,
):
    p_outs = rest[:8]
    cost_ref, p_ref, v_ref, v_send, g_send, a_ref, b_ref, sems, p_sems = rest[8:]

    def pack(ref, send_ref):
        for g in range(8):
            stack = jnp.concatenate([ref[g, :, a * 128 : a * 128 + 128] for a in range(4)], axis=0)
            turned = stack.T.reshape(16, 8, 128)
            for owner in range(16):
                send_ref[owner * 8 + g] = turned[owner]

    def get_u(m, half):
        g, cols = space_at(m)
        return tuple(u_ref[g, rows, cols] for rows in row_parts(half))

    cost = [jnp.zeros((8, 128), jnp.float32)]

    def put_u(m, half, values):
        g, cols = space_at(m)
        for part, rows in enumerate(row_parts(half)):
            p = values[0][part] + u_ref[g, rows, cols] * values[1][part]
            p_ref[g, rows, cols] = p
            v_ref[g, rows, cols] = values[1][part]
            cost[0] = cost[0] + p * p

    def get_p(m, half):
        g, cols = space_at(m)
        return tuple(p_ref[g, rows, cols] for rows in row_parts(half))

    def put_p(m, half, values):
        g, cols = space_at(m)
        for part, rows in enumerate(row_parts(half)):
            v_ref[g, rows, cols] = values[0][part] - u_ref[g, rows, cols] * values[1][part]

    symbol = space_symbol(scale_ref[0], small_ref)
    transform(get_u, put_u, 2, symbol, dft_ref, small_ref, a_ref, b_ref)
    cost_ref[...] = cost[0]
    copies = []
    for d in range(8):
        plane = (place_ref[0] + d) % 8
        copies.append(pltpu.make_async_copy(p_ref.at[plane], p_outs[d], p_sems.at[d]))
        copies[-1].start()
    pack(v_ref, v_send)
    copies.append(pltpu.make_async_copy(v_send, out_ref.at[:, 0:8, :], sems.at[0]))
    copies[-1].start()
    transform(get_p, put_p, 2, symbol, dft_ref, small_ref, a_ref, b_ref)
    pack(v_ref, g_send)
    copies.append(pltpu.make_async_copy(g_send, out_ref.at[:, 8:16, :], sems.at[1]))
    copies[-1].start()
    for copy in copies:
        copy.wait()


def time_first_kernel(
    scale_ref, place_ref, moved_ref, dft_ref, small_ref, u_ref, q_out, q_ref, a_ref, b_ref, sems
):
    for m in range(16):
        u_ref[m] = moved_ref[(place_ref[0] + 4 - m // 4) % 4, (place_ref[1] + 4 - m % 4) % 4]

    def get(m, half):
        t, cols = time_at(m)
        return tuple(u_ref[t, rows, cols] for rows in row_parts(half))

    def put(m, half, values):
        t, cols = time_at(m)
        for part, rows in enumerate(row_parts(half)):
            q_ref[t, rows, cols] = values[0][part]

    transform(get, put, 1, time_symbol(scale_ref[0], small_ref), dft_ref, small_ref, a_ref, b_ref)
    copy = pltpu.make_async_copy(q_ref, q_out, sems.at[0])
    copy.start()
    copy.wait()


def time_second_kernel(
    scale_ref,
    u_ref,
    q_in,
    recv_ref,
    cost_ref,
    dft_ref,
    small_ref,
    out_ref,
    q_ref,
    v_ref,
    s_ref,
    g_ref,
    sums_ref,
    a_ref,
    b_ref,
    sems,
):
    q_copy = pltpu.make_async_copy(q_in, q_ref, sems.at[0])
    q_copy.start()
    for m in range(16):
        for h in range(2):
            cols = slice(h * 128, h * 128 + 128)
            for o, ref in enumerate((v_ref, g_ref)):
                tiles = blocks4([recv_ref[m * 8 + 4 * h + k, 8 * o : 8 * o + 8] for k in range(4)])
                for a in range(4):
                    ref[m, 8 * a : 8 * a + 8, cols] = tiles[a]

    def get_v(m, half):
        t, cols = time_at(m)
        return tuple(v_ref[t, rows, cols] for rows in row_parts(half))

    def put_v(m, half, values):
        t, cols = time_at(m)
        for part, rows in enumerate(row_parts(half)):
            g_ref[t, rows, cols] = g_ref[t, rows, cols] - u_ref[t, rows, cols] * values[0][part]

    symbol = time_symbol(scale_ref[0], small_ref)
    transform(get_v, put_v, 1, symbol, dft_ref, small_ref, a_ref, b_ref)

    q_copy.wait()
    q_back = pltpu.make_async_copy(q_ref, out_ref.at[:, 0:32, :], sems.at[1])
    q_back.start()
    cost = 0.5 * cost_ref[...]
    for m in range(16):
        for h in range(2):
            cols = slice(h * 128, h * 128 + 128)
            for a in range(4):
                rows = slice(8 * a, 8 * a + 8)
                q = q_ref[m, rows, cols]
                w = u_ref[m, rows, cols] * v_ref[m, rows, cols]
                s_ref[m, rows, cols] = q + w
                cost = cost + q * (0.5 * q + w)
    norm = [jnp.zeros((8, 128), jnp.float32)]

    def get_s(m, half):
        t, cols = time_at(m)
        return tuple(s_ref[t, rows, cols] for rows in row_parts(half))

    def put_s(m, half, values):
        t, cols = time_at(m)
        for part, rows in enumerate(row_parts(half)):
            g = g_ref[t, rows, cols] - values[0][part]
            g_ref[t, rows, cols] = g
            norm[0] = norm[0] + g * g

    transform(get_s, put_s, 1, symbol, dft_ref, small_ref, a_ref, b_ref)
    g_back = pltpu.make_async_copy(g_ref, out_ref.at[:, 32:64, :], sems.at[2])
    g_back.start()
    for m in range(16):
        sums_ref[m, :, 0:128] = cost
        sums_ref[m, :, 128:256] = norm[0]
    sums_back = pltpu.make_async_copy(sums_ref, out_ref.at[:, 64:72, :], sems.at[3])
    sums_back.start()
    q_back.wait()
    g_back.wait()
    sums_back.wait()


def sums_kernel(recv_ref, out_ref):
    total = jnp.sum(recv_ref[...], axis=0)
    cost = jnp.sum(total[:, 0:128], axis=0, keepdims=True)
    norm = jnp.sum(total[:, 128:256], axis=0, keepdims=True)
    row = lax.broadcasted_iota(jnp.int32, (8, 128), 0)
    out_ref[...] = jnp.broadcast_to(jnp.where(row == 0, cost, norm)[None], (8, 8, 128))


def unturn(recv_ref, first, ref):
    for h in range(2):
        for a in range(4):
            rows = slice(first + 8 * a, first + 8 * a + 8)
            tile = recv_ref[:, rows, h * 128 : h * 128 + 128]
            ref[h * 128 : h * 128 + 128, a * 128 : a * 128 + 128] = tile.reshape(128, 128).T


def unturn_kernel(recv_ref, q_ref, g_ref):
    unturn(recv_ref, 0, q_ref)
    unturn(recv_ref, 32, g_ref)


def residual_kernel(place_ref, q_ref, *refs):
    r_ref = refs[8]
    for d in range(8):
        rows = pl.ds(pl.multiple_of((place_ref[0] + 8 - d) % 8 * 32, 32), 32)
        r_ref[rows, :] = q_ref[rows, :] + refs[d][...]


def update_kernel(u_ref, g_ref, sums_ref, out_ref):
    sums = jnp.sum(sums_ref[...], axis=0)
    cost = jnp.sum(sums[0:1, :], axis=1, keepdims=True)
    norm = jnp.sum(sums[1:2, :], axis=1, keepdims=True)
    out_ref[...] = u_ref[...] - (cost / (norm + GRAD_EPS)) * g_ref[...]


VM = pl.BlockSpec(memory_space=pltpu.VMEM)
SM = pl.BlockSpec(memory_space=pltpu.SMEM)
HB = pl.BlockSpec(memory_space=pl.ANY)


def f32(*shape):
    return jax.ShapeDtypeStruct(shape, jnp.float32)


def call(kernel, outs, ins, scratch=(), sems=(), flops=0):
    return pl.pallas_call(
        kernel,
        out_shape=[f32(*shape) for shape, _ in outs],
        in_specs=[spec for _, spec in ins],
        out_specs=[spec for _, spec in outs],
        scratch_shapes=[pltpu.VMEM(shape, jnp.float32) for shape in scratch]
        + [pltpu.SemaphoreType.DMA((count,)) for count in sems],
        cost_estimate=pl.CostEstimate(flops=flops, bytes_accessed=2**21, transcendentals=0),
        compiler_params=pltpu.CompilerParams(vmem_limit_bytes=VMEM_LIMIT),
    )(*[array for array, _ in ins])


def shift_pairs(axis, shift):
    pairs = []
    for y in range(4):
        for x in range(4):
            to = (y, (x + shift) % 4) if axis else ((y + shift) % 4, x)
            pairs.append((4 * y + x, 4 * to[0] + to[1]))
    return pairs


def along_x(turned, x):
    pieces = turned.reshape(4, 4, 32, 256)
    moved = []
    for d in range(4):
        piece = lax.dynamic_index_in_dim(pieces, (x + d) % 4, 1, keepdims=False)
        moved.append(lax.ppermute(piece, "ta", shift_pairs(1, d)) if d else piece)
    return moved


def along_y(pieces, y):
    moved = []
    for e in range(4):
        piece = jnp.stack(
            [lax.dynamic_index_in_dim(part, (y + e) % 4, 0, keepdims=False) for part in pieces]
        )
        moved.append(lax.ppermute(piece, "ta", shift_pairs(0, e)) if e else piece)
    return jnp.stack(moved)


def local(field, time_period, space_period):
    dft_np, small_np = np_tables()
    dft = (jnp.asarray(dft_np), VM)
    small = (jnp.asarray(small_np), VM)
    time_scale = (TWO_PI / time_period, SM)
    space_scale = (TWO_PI / space_period, SM)
    rows, cols = (8, 32, 512), (16, 32, 256)
    planes = (RADIX, 16, 2 * SUB)
    here = lax.axis_index("ta")
    y, x = here // 4, here % 4
    z = lax.axis_index("gx")
    z_place = (z.reshape(1), SM)
    t_place = (jnp.stack([y, x]), SM)

    rows_u = lax.all_to_all(field.reshape(rows), "gx", 0, 0)
    (turned,) = call(turn_kernel, [(cols, VM)], [(field, VM)])
    first_move = along_x(turned, x)
    pieces, *p_planes, p_cost = call(
        space_kernel,
        [((128, 16, 128), HB)] + [((32, 512), HB)] * 8 + [((8, 128), VM)],
        [space_scale, z_place, (rows_u, VM), dft, small],
        [rows, rows, (128, 8, 128), (128, 8, 128), planes, (2, *planes)],
        [2, 8],
        flops=8 * 10**9,
    )
    pieces, first_move = lax.optimization_barrier((pieces, first_move))
    received = lax.all_to_all(pieces, ("ta", "gx"), 0, 0)
    moved = along_y(first_move, y)
    cols_u, cols_q = call(
        time_first_kernel,
        [(cols, VM), (cols, HB)],
        [time_scale, t_place, (moved, VM), dft, small],
        [cols, planes, (1, *planes)],
        [1],
        flops=2 * 10**9,
    )
    (cols_out,) = call(
        time_second_kernel,
        [((16, 72, 256), HB)],
        [time_scale, (cols_u, VM), (cols_q, HB), (received, VM), (p_cost, VM), dft, small],
        [cols, cols, cols, cols, (16, 8, 256), planes, (1, *planes)],
        [4],
        flops=4 * 10**9,
    )
    cols_out, p_planes = lax.optimization_barrier((cols_out, p_planes))
    back = lax.all_to_all(cols_out, "ta", 0, 0)
    p_block = [
        lax.ppermute(plane, "gx", [(i, (i + d) % 8) for i in range(8)]) if d else plane
        for d, plane in enumerate(p_planes)
    ]
    (sums,) = call(sums_kernel, [((8, 8, 128), VM)], [(back[:, 64:72, :], VM)])
    sums = lax.all_to_all(sums, "gx", 0, 0)
    block_q, block_g = call(unturn_kernel, [((256, 512), VM), ((256, 512), VM)], [(back, VM)])
    (residual,) = call(
        residual_kernel,
        [((256, 512), VM)],
        [z_place, (block_q, VM)] + [(plane, VM) for plane in p_block],
    )
    (updated,) = call(
        update_kernel, [((256, 512), VM)], [(field, VM), (block_g, VM), (sums, VM)]
    )
    return updated, residual


def solution(mesh):
    placed = (P(("tile", "ta"), "gx"), P("tile"), P("tile"))
    return jax.shard_map(
        local,
        mesh=mesh,
        in_specs=placed,
        out_specs=(P(("tile", "ta"), "gx"), P(("tile", "ta"), "gx")),
        check_vma=False,
    )
```

```python
import math

import jax
import jax.numpy as jnp
import ml_dtypes
import numpy as np
from jax import lax
from jax.experimental import pallas as pl
from jax.experimental.pallas import tpu as pltpu
from jax.sharding import PartitionSpec as P

TWO_PI = 2.0 * math.pi
GRAD_EPS = 1e-06
LEN = 4096
RADIX = 32
SUB = 128
PARTS = 3
GROUP = 8
VMEM_LIMIT = 24 * 1024 * 1024


def np_parts(values):
    rest = np.asarray(values, np.float64)
    parts = []
    for _ in range(PARTS):
        part = rest.astype(np.float32).astype(ml_dtypes.bfloat16)
        parts.append(part)
        rest = rest - part.astype(np.float64)
    return parts


def np_tables():
    j = np.arange(SUB)
    angle = TWO_PI * (np.outer(j, j) % SUB) / SUB
    cos, sin = np.cos(angle), np.sin(angle)
    dft = np.stack(np_parts(np.block([[cos, -sin], [sin, cos]])))
    k1 = np.arange(RADIX)
    twist = TWO_PI * np.outer(k1, j) / LEN
    mode = k1[:, None] + RADIX * j[None, :]
    signed = np.where(mode < LEN // 2, mode, mode - LEN)
    odd = np.where(mode == LEN // 2, 0, signed)
    small = np.stack([np.cos(twist), np.sin(twist), signed, odd]).astype(np.float32)
    return dft, small


def cadd(a, b):
    return (a[0] + b[0], a[1] + b[1])


def csub(a, b):
    return (a[0] - b[0], a[1] - b[1])


def dft4(x, sign):
    s = cadd(x[0], x[2])
    d = csub(x[0], x[2])
    t = cadd(x[1], x[3])
    e = csub(x[1], x[3])
    if sign < 0:
        ie = (e[1], -e[0])
    else:
        ie = (-e[1], e[0])
    return [cadd(s, t), cadd(d, ie), csub(s, t), csub(d, ie)]


def crot(x, turns, sign):
    turns = turns % 32
    if turns == 0:
        return x
    if turns == 8:
        return (x[1], -x[0]) if sign < 0 else (-x[1], x[0])
    c = math.cos(TWO_PI * turns / 32)
    s = sign * math.sin(TWO_PI * turns / 32)
    if turns == 4:
        return ((x[0] - sign * x[1]) * c, (x[1] + sign * x[0]) * c)
    if turns == 12:
        return ((x[0] + sign * x[1]) * c, (x[1] - sign * x[0]) * c)
    return (x[0] * c - x[1] * s, x[0] * s + x[1] * c)


def dft8(x, sign):
    even = dft4(x[0::2], sign)
    odd = [crot(value, 4 * k, sign) for k, value in enumerate(dft4(x[1::2], sign))]
    return [cadd(even[k], odd[k]) for k in range(4)] + [csub(even[k], odd[k]) for k in range(4)]


def dft32(x, sign):
    out = [None] * 32
    rows = []
    for n2 in range(8):
        y = dft4([x(8 * n1 + n2) for n1 in range(4)], sign)
        rows.append([crot(y[k1], n2 * k1, sign) for k1 in range(4)])
    for k1 in range(4):
        z = dft8([rows[n2][k1] for n2 in range(8)], sign)
        for k2 in range(8):
            out[k1 + 4 * k2] = z[k2]
    return out


def product(values, table_ref):
    parts = []
    rest = values
    for step in range(PARTS):
        part = rest.astype(jnp.bfloat16)
        parts.append(part)
        if step < PARTS - 1:
            rest = rest - part.astype(jnp.float32)
    order = [(i, k - i) for k in reversed(range(PARTS)) for i in range(k + 1)]
    left = jnp.concatenate([parts[i] for i, _ in order], axis=1)
    right = jnp.concatenate([table_ref[j] for _, j in order], axis=0)
    return jnp.dot(left, right, preferred_element_type=jnp.float32)


def transform(get, put, outputs, symbol, dft_ref, small_ref, a_ref, b_ref):
    re_lanes, im_lanes = slice(0, SUB), slice(SUB, 2 * SUB)
    for half in range(2):
        rows = slice(8 * half, 8 * half + 8)
        planes = dft32(lambda m: get(m, half), -1)
        for k1 in range(RADIX):
            re, im = planes[k1]
            if k1:
                c = small_ref[0, k1 : k1 + 1, :]
                s = small_ref[1, k1 : k1 + 1, :]
                re, im = re * c + im * s, im * c - re * s
            a_ref[k1, rows, re_lanes] = re
            a_ref[k1, rows, im_lanes] = im
    for group in range(RADIX // GROUP):
        ks = slice(group * GROUP, (group + 1) * GROUP)
        got = product(a_ref[ks].reshape(GROUP * 16, 2 * SUB), dft_ref)
        got = got.reshape(GROUP, 16, 2 * SUB)
        re, im = got[:, :, re_lanes], got[:, :, im_lanes]
        for o in range(outputs):
            swapped = jnp.concatenate(symbol(o, ks, re, im)[::-1], axis=2)
            got = product(swapped.reshape(GROUP * 16, 2 * SUB), dft_ref)
            got = got.reshape(GROUP, 16, 2 * SUB)
            im2, re2 = got[:, :, re_lanes], got[:, :, im_lanes]
            c = small_ref[0, ks][:, None, :]
            s = small_ref[1, ks][:, None, :]
            b_ref[o, ks, :, re_lanes] = re2 * c - im2 * s
            b_ref[o, ks, :, im_lanes] = im2 * c + re2 * s
    for half in range(2):
        rows = slice(8 * half, 8 * half + 8)
        outs = [
            dft32(lambda k: (b_ref[o, k, rows, re_lanes], b_ref[o, k, rows, im_lanes]), 1)
            for o in range(outputs)
        ]
        for m in range(RADIX):
            put(m, half, [outs[o][m] for o in range(outputs)])


def space_symbol(scale, small_ref):
    def symbol(o, ks, re, im):
        if o == 0:
            wave = small_ref[2, ks] * scale
            square = wave * wave
            even = ((square * square - square) * (1.0 / LEN))[:, None, :]
            return re * even, im * even
        odd = (small_ref[3, ks] * (scale * (1.0 / LEN)))[:, None, :]
        return -im * odd, re * odd

    return symbol


def time_symbol(scale, small_ref):
    def symbol(o, ks, re, im):
        odd = (small_ref[3, ks] * (scale * (1.0 / LEN)))[:, None, :]
        return -im * odd, re * odd

    return symbol


def row_parts(half):
    return slice(8 * half, 8 * half + 8), slice(16 + 8 * half, 24 + 8 * half)


def space_at(m):
    return m // 4, slice((m % 4) * 128, (m % 4) * 128 + 128)


def time_at(m):
    return m // 2, slice((m % 2) * 128, (m % 2) * 128 + 128)


def blocks4(tiles):
    lane = lax.broadcasted_iota(jnp.int32, tiles[0].shape, len(tiles[0].shape) - 1)
    axis = len(tiles[0].shape) - 1
    low_half = lane < 64
    even = (lane // 32) % 2 == 0

    def swap(x, y, shift, mask):
        first = jnp.where(mask, x, pltpu.roll(y, shift, axis))
        second = jnp.where(mask, pltpu.roll(x, 128 - shift, axis), y)
        return first, second

    t0, t2 = swap(tiles[0], tiles[2], 64, low_half)
    t1, t3 = swap(tiles[1], tiles[3], 64, low_half)
    t0, t1 = swap(t0, t1, 32, even)
    t2, t3 = swap(t2, t3, 32, even)
    return [t0, t1, t2, t3]


def turn_kernel(u_ref, out_ref):
    for h in range(2):
        for a in range(4):
            tile = u_ref[h * 128 : h * 128 + 128, a * 128 : a * 128 + 128].T
            out_ref[:, a * 8 : a * 8 + 8, h * 128 : h * 128 + 128] = tile.reshape(16, 8, 128)


def fold(values):
    lanes = sum(values[:, a * 128 : a * 128 + 128] for a in range(4))
    return sum(lanes[8 * a : 8 * a + 8] for a in range(4))


def space_kernel(
    scale_ref,
    place_ref,
    u_ref,
    dft_ref,
    small_ref,
    out_ref,
    *rest,
):
    p_outs = rest[:8]
    cost_ref, p_ref, v_ref, v_send, g_send, a_ref, b_ref, sems, p_sems = rest[8:]

    def pack(ref, send_ref):
        for g in range(8):
            stack = jnp.concatenate([ref[g, :, a * 128 : a * 128 + 128] for a in range(4)], axis=0)
            turned = stack.T.reshape(16, 8, 128)
            for owner in range(16):
                send_ref[owner * 8 + g] = turned[owner]

    def get_u(m, half):
        g, cols = space_at(m)
        return tuple(u_ref[g, rows, cols] for rows in row_parts(half))

    def put_u(m, half, values):
        g, cols = space_at(m)
        for part, rows in enumerate(row_parts(half)):
            p = values[0][part] + u_ref[g, rows, cols] * values[1][part]
            p_ref[g, rows, cols] = p
            v_ref[g, rows, cols] = values[1][part]

    def get_p(m, half):
        g, cols = space_at(m)
        return tuple(p_ref[g, rows, cols] for rows in row_parts(half))

    def put_p(m, half, values):
        g, cols = space_at(m)
        for part, rows in enumerate(row_parts(half)):
            v_ref[g, rows, cols] = values[0][part] - u_ref[g, rows, cols] * values[1][part]

    symbol = space_symbol(scale_ref[0], small_ref)
    transform(get_u, put_u, 2, symbol, dft_ref, small_ref, a_ref, b_ref)
    copies = []
    for d in range(8):
        plane = (place_ref[0] + d) % 8
        copies.append(pltpu.make_async_copy(p_ref.at[plane], p_outs[d], p_sems.at[d]))
        copies[-1].start()
    cost_ref[...] = fold(jnp.sum(p_ref[...] * p_ref[...], axis=0))
    pack(v_ref, v_send)
    copies.append(pltpu.make_async_copy(v_send, out_ref.at[:, 0:8, :], sems.at[0]))
    copies[-1].start()
    transform(get_p, put_p, 2, symbol, dft_ref, small_ref, a_ref, b_ref)
    pack(v_ref, g_send)
    copies.append(pltpu.make_async_copy(g_send, out_ref.at[:, 8:16, :], sems.at[1]))
    copies[-1].start()
    for copy in copies:
        copy.wait()


def time_first_kernel(scale_ref, place_ref, moved_ref, dft_ref, small_ref, uq_ref, a_ref, b_ref):
    for m in range(16):
        uq_ref[0, m] = moved_ref[(place_ref[0] + 4 - m // 4) % 4, (place_ref[1] + 4 - m % 4) % 4]

    def get(m, half):
        t, cols = time_at(m)
        return tuple(uq_ref[0, t, rows, cols] for rows in row_parts(half))

    def put(m, half, values):
        t, cols = time_at(m)
        for part, rows in enumerate(row_parts(half)):
            uq_ref[1, t, rows, cols] = values[0][part]

    transform(get, put, 1, time_symbol(scale_ref[0], small_ref), dft_ref, small_ref, a_ref, b_ref)


def time_second_kernel(
    scale_ref,
    uq_ref,
    recv_ref,
    p_cost_ref,
    dft_ref,
    small_ref,
    out_ref,
    v_ref,
    s_ref,
    g_ref,
    sums_ref,
    a_ref,
    b_ref,
    sems,
):
    copies = [pltpu.make_async_copy(uq_ref.at[1], out_ref.at[:, 0:32, :], sems.at[0])]
    copies[-1].start()
    costs = [jnp.zeros((8, 128), jnp.float32)] * 8
    for m in range(16):
        for h in range(2):
            cols = slice(h * 128, h * 128 + 128)
            for o, ref in enumerate((v_ref, g_ref)):
                tiles = blocks4([recv_ref[m * 8 + 4 * h + k, 8 * o : 8 * o + 8] for k in range(4)])
                for a in range(4):
                    rows = slice(8 * a, 8 * a + 8)
                    ref[m, rows, cols] = tiles[a]
                    if o == 0:
                        q = uq_ref[1, m, rows, cols]
                        w = uq_ref[0, m, rows, cols] * tiles[a]
                        s_ref[m, rows, cols] = q + w
                        costs[4 * h + a] = costs[4 * h + a] + q * (0.5 * q + w)

    def get_v(m, half):
        t, cols = time_at(m)
        return tuple(v_ref[t, rows, cols] for rows in row_parts(half))

    def put_v(m, half, values):
        t, cols = time_at(m)
        for part, rows in enumerate(row_parts(half)):
            v_ref[t, rows, cols] = (
                g_ref[t, rows, cols] - uq_ref[0, t, rows, cols] * values[0][part]
            )

    norms = [jnp.zeros((8, 128), jnp.float32)] * 8

    def get_s(m, half):
        t, cols = time_at(m)
        return tuple(s_ref[t, rows, cols] for rows in row_parts(half))

    def put_s(m, half, values):
        t, cols = time_at(m)
        for part, rows in enumerate(row_parts(half)):
            g = v_ref[t, rows, cols] - values[0][part]
            g_ref[t, rows, cols] = g
            slot = 2 * (m % 4) + part
            norms[slot] = norms[slot] + g * g

    symbol = time_symbol(scale_ref[0], small_ref)
    transform(get_v, put_v, 1, symbol, dft_ref, small_ref, a_ref, b_ref)
    transform(get_s, put_s, 1, symbol, dft_ref, small_ref, a_ref, b_ref)
    copies.append(pltpu.make_async_copy(g_ref, out_ref.at[:, 32:64, :], sems.at[1]))
    copies[-1].start()
    cost = sum(costs) + 0.5 * p_cost_ref[...]
    norm = sum(norms)
    for m in range(16):
        sums_ref[m, :, 0:128] = cost
        sums_ref[m, :, 128:256] = norm
    copies.append(pltpu.make_async_copy(sums_ref, out_ref.at[:, 64:72, :], sems.at[2]))
    copies[-1].start()
    for copy in copies:
        copy.wait()


def sums_kernel(recv_ref, out_ref):
    total = jnp.sum(recv_ref[...], axis=0)
    cost = jnp.sum(total[:, 0:128], axis=0, keepdims=True)
    norm = jnp.sum(total[:, 128:256], axis=0, keepdims=True)
    row = lax.broadcasted_iota(jnp.int32, (8, 128), 0)
    out_ref[...] = jnp.broadcast_to(jnp.where(row == 0, cost, norm)[None], (8, 8, 128))


def unturn(recv_ref, first, ref):
    for h in range(2):
        for a in range(4):
            rows = slice(first + 8 * a, first + 8 * a + 8)
            tile = recv_ref[:, rows, h * 128 : h * 128 + 128]
            ref[h * 128 : h * 128 + 128, a * 128 : a * 128 + 128] = tile.reshape(128, 128).T


def unturn_kernel(recv_ref, q_ref, g_ref):
    unturn(recv_ref, 0, q_ref)
    unturn(recv_ref, 32, g_ref)


def residual_kernel(place_ref, q_ref, *refs):
    r_ref = refs[8]
    for d in range(8):
        rows = pl.ds(pl.multiple_of((place_ref[0] + 8 - d) % 8 * 32, 32), 32)
        r_ref[rows, :] = q_ref[rows, :] + refs[d][...]


def update_kernel(u_ref, g_ref, sums_ref, out_ref):
    sums = jnp.sum(sums_ref[...], axis=0)
    cost = jnp.sum(sums[0:1, :], axis=1, keepdims=True)
    norm = jnp.sum(sums[1:2, :], axis=1, keepdims=True)
    out_ref[...] = u_ref[...] - (cost / (norm + GRAD_EPS)) * g_ref[...]


VM = pl.BlockSpec(memory_space=pltpu.VMEM)
SM = pl.BlockSpec(memory_space=pltpu.SMEM)
HB = pl.BlockSpec(memory_space=pl.ANY)


def f32(*shape):
    return jax.ShapeDtypeStruct(shape, jnp.float32)


def call(kernel, outs, ins, scratch=(), sems=(), flops=0):
    return pl.pallas_call(
        kernel,
        out_shape=[f32(*shape) for shape, _ in outs],
        in_specs=[spec for _, spec in ins],
        out_specs=[spec for _, spec in outs],
        scratch_shapes=[pltpu.VMEM(shape, jnp.float32) for shape in scratch]
        + [pltpu.SemaphoreType.DMA((count,)) for count in sems],
        cost_estimate=pl.CostEstimate(flops=flops, bytes_accessed=2**21, transcendentals=0),
        compiler_params=pltpu.CompilerParams(vmem_limit_bytes=VMEM_LIMIT),
    )(*[array for array, _ in ins])


def shift_pairs(axis, shift):
    pairs = []
    for y in range(4):
        for x in range(4):
            to = (y, (x + shift) % 4) if axis else ((y + shift) % 4, x)
            pairs.append((4 * y + x, 4 * to[0] + to[1]))
    return pairs


def along_x(turned, x):
    pieces = turned.reshape(4, 4, 32, 256)
    moved = []
    for d in range(4):
        piece = lax.dynamic_index_in_dim(pieces, (x + d) % 4, 1, keepdims=False)
        moved.append(lax.ppermute(piece, "ta", shift_pairs(1, d)) if d else piece)
    return moved


def along_y(pieces, y):
    moved = []
    for e in range(4):
        piece = jnp.stack(
            [lax.dynamic_index_in_dim(part, (y + e) % 4, 0, keepdims=False) for part in pieces]
        )
        moved.append(lax.ppermute(piece, "ta", shift_pairs(0, e)) if e else piece)
    return jnp.stack(moved)


def local(field, time_period, space_period):
    dft_np, small_np = np_tables()
    dft = (jnp.asarray(dft_np), VM)
    small = (jnp.asarray(small_np), VM)
    time_scale = (TWO_PI / time_period, SM)
    space_scale = (TWO_PI / space_period, SM)
    rows, cols = (8, 32, 512), (16, 32, 256)
    planes = (RADIX, 16, 2 * SUB)
    here = lax.axis_index("ta")
    y, x = here // 4, here % 4
    z = lax.axis_index("gx")
    z_place = (z.reshape(1), SM)
    t_place = (jnp.stack([y, x]), SM)

    rows_u = lax.all_to_all(field.reshape(rows), "gx", 0, 0)
    (turned,) = call(turn_kernel, [(cols, VM)], [(field, VM)])
    first_move = along_x(turned, x)
    pieces, *p_planes, p_cost = call(
        space_kernel,
        [((128, 16, 128), HB)] + [((32, 512), HB)] * 8 + [((8, 128), VM)],
        [space_scale, z_place, (rows_u, VM), dft, small],
        [rows, rows, (128, 8, 128), (128, 8, 128), planes, (2, *planes)],
        [2, 8],
        flops=8 * 10**9,
    )
    pieces, first_move = lax.optimization_barrier((pieces, first_move))
    received = lax.all_to_all(pieces, ("ta", "gx"), 0, 0)
    moved = along_y(first_move, y)
    (cols_uq,) = call(
        time_first_kernel,
        [((2, *cols), VM)],
        [time_scale, t_place, (moved, VM), dft, small],
        [planes, (1, *planes)],
        flops=2 * 10**9,
    )
    (cols_out,) = call(
        time_second_kernel,
        [((16, 72, 256), HB)],
        [time_scale, (cols_uq, VM), (received, VM), (p_cost, VM), dft, small],
        [cols, cols, cols, (16, 8, 256), planes, (1, *planes)],
        [3],
        flops=4 * 10**9,
    )
    cols_out, p_planes = lax.optimization_barrier((cols_out, p_planes))
    back = lax.all_to_all(cols_out, "ta", 0, 0)
    p_block = [
        lax.ppermute(plane, "gx", [(i, (i + d) % 8) for i in range(8)]) if d else plane
        for d, plane in enumerate(p_planes)
    ]
    (sums,) = call(sums_kernel, [((8, 8, 128), VM)], [(back[:, 64:72, :], VM)])
    sums = lax.all_to_all(sums, "gx", 0, 0)
    block_q, block_g = call(unturn_kernel, [((256, 512), VM), ((256, 512), VM)], [(back, VM)])
    (residual,) = call(
        residual_kernel,
        [((256, 512), VM)],
        [z_place, (block_q, VM)] + [(plane, VM) for plane in p_block],
    )
    (updated,) = call(
        update_kernel, [((256, 512), VM)], [(field, VM), (block_g, VM), (sums, VM)]
    )
    return updated, residual


def solution(mesh):
    placed = (P(("tile", "ta"), "gx"), P("tile"), P("tile"))
    return jax.shard_map(
        local,
        mesh=mesh,
        in_specs=placed,
        out_specs=(P(("tile", "ta"), "gx"), P(("tile", "ta"), "gx")),
        check_vma=False,
    )
```

```python
import math

import jax
import jax.numpy as jnp
import ml_dtypes
import numpy as np
from jax import lax
from jax.experimental import pallas as pl
from jax.experimental.pallas import tpu as pltpu
from jax.sharding import PartitionSpec as P

TWO_PI = 2.0 * math.pi
GRAD_EPS = 1e-06
LEN = 4096
RADIX = 32
SUB = 128
PARTS = 3
SPACE_GROUP = 32
TIME_GROUP = 8
VMEM_LIMIT = 24 * 1024 * 1024


def np_parts(values):
    rest = np.asarray(values, np.float64)
    parts = []
    for _ in range(PARTS):
        part = rest.astype(np.float32).astype(ml_dtypes.bfloat16)
        parts.append(part)
        rest = rest - part.astype(np.float64)
    return parts


def np_tables():
    j = np.arange(SUB)
    angle = TWO_PI * (np.outer(j, j) % SUB) / SUB
    cos, sin = np.cos(angle), np.sin(angle)
    dft = np.stack(np_parts(np.block([[cos, -sin], [sin, cos]])))
    k1 = np.arange(RADIX)
    twist = TWO_PI * np.outer(k1, j) / LEN
    mode = k1[:, None] + RADIX * j[None, :]
    signed = np.where(mode < LEN // 2, mode, mode - LEN)
    odd = np.where(mode == LEN // 2, 0, signed)
    small = np.stack([np.cos(twist), np.sin(twist), signed, odd]).astype(np.float32)
    return dft, small


def cadd(a, b):
    return (a[0] + b[0], a[1] + b[1])


def csub(a, b):
    return (a[0] - b[0], a[1] - b[1])


def dft4(x, sign):
    s = cadd(x[0], x[2])
    d = csub(x[0], x[2])
    t = cadd(x[1], x[3])
    e = csub(x[1], x[3])
    if sign < 0:
        ie = (e[1], -e[0])
    else:
        ie = (-e[1], e[0])
    return [cadd(s, t), cadd(d, ie), csub(s, t), csub(d, ie)]


def crot(x, turns, sign):
    turns = turns % 32
    if turns == 0:
        return x
    if turns == 8:
        return (x[1], -x[0]) if sign < 0 else (-x[1], x[0])
    c = math.cos(TWO_PI * turns / 32)
    s = sign * math.sin(TWO_PI * turns / 32)
    if turns == 4:
        return ((x[0] - sign * x[1]) * c, (x[1] + sign * x[0]) * c)
    if turns == 12:
        return ((x[0] + sign * x[1]) * c, (x[1] - sign * x[0]) * c)
    return (x[0] * c - x[1] * s, x[0] * s + x[1] * c)


def dft8(x, sign):
    even = dft4(x[0::2], sign)
    odd = [crot(value, 4 * k, sign) for k, value in enumerate(dft4(x[1::2], sign))]
    return [cadd(even[k], odd[k]) for k in range(4)] + [csub(even[k], odd[k]) for k in range(4)]


def dft32(x, sign):
    out = [None] * 32
    rows = []
    for n2 in range(8):
        y = dft4([x(8 * n1 + n2) for n1 in range(4)], sign)
        rows.append([crot(y[k1], n2 * k1, sign) for k1 in range(4)])
    for k1 in range(4):
        z = dft8([rows[n2][k1] for n2 in range(8)], sign)
        for k2 in range(8):
            out[k1 + 4 * k2] = z[k2]
    return out


def product(values, table_ref):
    parts = []
    rest = values
    for step in range(PARTS):
        part = rest.astype(jnp.bfloat16)
        parts.append(part)
        if step < PARTS - 1:
            rest = rest - part.astype(jnp.float32)
    order = [(i, k - i) for k in reversed(range(PARTS)) for i in range(k + 1)]
    left = jnp.concatenate([parts[i] for i, _ in order], axis=1)
    right = jnp.concatenate([table_ref[j] for _, j in order], axis=0)
    return jnp.dot(left, right, preferred_element_type=jnp.float32)


def transform(get, put, outputs, symbol, dft_ref, small_ref, a_ref, b_ref, group, after=None):
    re_lanes, im_lanes = slice(0, SUB), slice(SUB, 2 * SUB)
    for half in range(2):
        rows = slice(8 * half, 8 * half + 8)
        planes = dft32(lambda m: get(m, half), -1)
        for k1 in range(RADIX):
            re, im = planes[k1]
            if k1:
                c = small_ref[0, k1 : k1 + 1, :]
                s = small_ref[1, k1 : k1 + 1, :]
                re, im = re * c + im * s, im * c - re * s
            a_ref[k1, rows, re_lanes] = re
            a_ref[k1, rows, im_lanes] = im
    for first in range(0, RADIX, group):
        ks = slice(first, first + group)
        got = product(a_ref[ks].reshape(group * 16, 2 * SUB), dft_ref)
        got = got.reshape(group, 16, 2 * SUB)
        re, im = got[:, :, re_lanes], got[:, :, im_lanes]
        for o in range(outputs):
            swapped = jnp.concatenate(symbol(o, ks, re, im)[::-1], axis=2)
            got = product(swapped.reshape(group * 16, 2 * SUB), dft_ref)
            got = got.reshape(group, 16, 2 * SUB)
            im2, re2 = got[:, :, re_lanes], got[:, :, im_lanes]
            c = small_ref[0, ks][:, None, :]
            s = small_ref[1, ks][:, None, :]
            b_ref[o, ks, :, re_lanes] = re2 * c - im2 * s
            b_ref[o, ks, :, im_lanes] = im2 * c + re2 * s
    for half in range(2):
        rows = slice(8 * half, 8 * half + 8)
        outs = [
            dft32(lambda k: (b_ref[o, k, rows, re_lanes], b_ref[o, k, rows, im_lanes]), 1)
            for o in range(outputs)
        ]
        for m in range(RADIX):
            put(m, half, [outs[o][m] for o in range(outputs)])
        if after is not None:
            after(half)


def space_symbol(scale, small_ref):
    def symbol(o, ks, re, im):
        if o == 0:
            wave = small_ref[2, ks] * scale
            square = wave * wave
            even = ((square * square - square) * (1.0 / LEN))[:, None, :]
            return re * even, im * even
        odd = (small_ref[3, ks] * (scale * (1.0 / LEN)))[:, None, :]
        return -im * odd, re * odd

    return symbol


def time_symbol(scale, small_ref):
    def symbol(o, ks, re, im):
        odd = (small_ref[3, ks] * (scale * (1.0 / LEN)))[:, None, :]
        return -im * odd, re * odd

    return symbol


def row_parts(half):
    return slice(8 * half, 8 * half + 8), slice(16 + 8 * half, 24 + 8 * half)


def space_at(m):
    return m // 4, slice((m % 4) * 128, (m % 4) * 128 + 128)


def time_at(m):
    return m // 2, slice((m % 2) * 128, (m % 2) * 128 + 128)


def blocks4(tiles):
    lane = lax.broadcasted_iota(jnp.int32, tiles[0].shape, len(tiles[0].shape) - 1)
    axis = len(tiles[0].shape) - 1
    low_half = lane < 64
    even = (lane // 32) % 2 == 0

    def swap(x, y, shift, mask):
        first = jnp.where(mask, x, pltpu.roll(y, shift, axis))
        second = jnp.where(mask, pltpu.roll(x, 128 - shift, axis), y)
        return first, second

    t0, t2 = swap(tiles[0], tiles[2], 64, low_half)
    t1, t3 = swap(tiles[1], tiles[3], 64, low_half)
    t0, t1 = swap(t0, t1, 32, even)
    t2, t3 = swap(t2, t3, 32, even)
    return [t0, t1, t2, t3]


def turn_kernel(u_ref, out_ref):
    for h in range(2):
        for a in range(4):
            tile = u_ref[h * 128 : h * 128 + 128, a * 128 : a * 128 + 128].T
            out_ref[:, a * 8 : a * 8 + 8, h * 128 : h * 128 + 128] = tile.reshape(16, 8, 128)


def fold(values):
    lanes = sum(values[:, a * 128 : a * 128 + 128] for a in range(4))
    return sum(lanes[8 * a : 8 * a + 8] for a in range(4))


def space_kernel(
    scale_ref,
    place_ref,
    u_ref,
    dft_ref,
    small_ref,
    out_ref,
    *rest,
):
    p_outs = rest[:8]
    cost_ref, p_ref, v_ref, send_ref, a_ref, b_ref, sems, p_sems = rest[8:]

    def pack(ref, g, slot):
        stack = jnp.concatenate([ref[g, :, a * 128 : a * 128 + 128] for a in range(4)], axis=0)
        send_ref[g, :, 8 * slot : 8 * slot + 8, :] = stack.T.reshape(16, 8, 128)

    def get_u(m, half):
        g, cols = space_at(m)
        return tuple(u_ref[g, rows, cols] for rows in row_parts(half))

    def put_u(m, half, values):
        g, cols = space_at(m)
        for part, rows in enumerate(row_parts(half)):
            p = values[0][part] + u_ref[g, rows, cols] * values[1][part]
            p_ref[g, rows, cols] = p
            v_ref[g, rows, cols] = values[1][part]

    def get_p(m, half):
        g, cols = space_at(m)
        return tuple(p_ref[g, rows, cols] for rows in row_parts(half))

    def put_p(m, half, values):
        g, cols = space_at(m)
        for part, rows in enumerate(row_parts(half)):
            v_ref[g, rows, cols] = values[0][part] - u_ref[g, rows, cols] * values[1][part]

    symbol = space_symbol(scale_ref[0], small_ref)
    transform(get_u, put_u, 2, symbol, dft_ref, small_ref, a_ref, b_ref, SPACE_GROUP)
    copies = []
    for d in range(8):
        plane = (place_ref[0] + d) % 8
        copies.append(pltpu.make_async_copy(p_ref.at[plane], p_outs[d], p_sems.at[d]))
        copies[-1].start()
    cost_ref[...] = fold(jnp.sum(p_ref[...] * p_ref[...], axis=0))
    for g in range(8):
        pack(v_ref, g, 0)
    transform(get_p, put_p, 2, symbol, dft_ref, small_ref, a_ref, b_ref, SPACE_GROUP)
    for g in range(8):
        pack(v_ref, g, 1)
        copies.append(pltpu.make_async_copy(send_ref.at[g], out_ref.at[g], sems.at[g]))
        copies[-1].start()
    for copy in copies:
        copy.wait()


def time_first_kernel(scale_ref, place_ref, moved_ref, dft_ref, small_ref, uq_ref, a_ref, b_ref):
    for m in range(16):
        uq_ref[0, m] = moved_ref[(place_ref[0] + 4 - m // 4) % 4, (place_ref[1] + 4 - m % 4) % 4]

    def get(m, half):
        t, cols = time_at(m)
        return tuple(uq_ref[0, t, rows, cols] for rows in row_parts(half))

    def put(m, half, values):
        t, cols = time_at(m)
        for part, rows in enumerate(row_parts(half)):
            uq_ref[1, t, rows, cols] = values[0][part]

    symbol = time_symbol(scale_ref[0], small_ref)
    transform(get, put, 1, symbol, dft_ref, small_ref, a_ref, b_ref, TIME_GROUP)


def time_second_kernel(
    scale_ref,
    uq_ref,
    recv_ref,
    p_cost_ref,
    dft_ref,
    small_ref,
    out_ref,
    v_ref,
    s_ref,
    g_ref,
    sums_ref,
    a_ref,
    b_ref,
    sems,
):
    copies = [pltpu.make_async_copy(uq_ref.at[1], out_ref.at[:, 0:32, :], sems.at[0])]
    copies[-1].start()
    costs = [jnp.zeros((8, 128), jnp.float32)] * 8
    for m in range(16):
        for h in range(2):
            cols = slice(h * 128, h * 128 + 128)
            for o, ref in enumerate((v_ref, g_ref)):
                tiles = blocks4([recv_ref[(4 * h + k) * 16 + m, 8 * o : 8 * o + 8] for k in range(4)])
                for a in range(4):
                    rows = slice(8 * a, 8 * a + 8)
                    ref[m, rows, cols] = tiles[a]
                    if o == 0:
                        q = uq_ref[1, m, rows, cols]
                        w = uq_ref[0, m, rows, cols] * tiles[a]
                        s_ref[m, rows, cols] = q + w
                        costs[4 * h + a] = costs[4 * h + a] + q * (0.5 * q + w)

    def get_v(m, half):
        t, cols = time_at(m)
        return tuple(v_ref[t, rows, cols] for rows in row_parts(half))

    def put_v(m, half, values):
        t, cols = time_at(m)
        for part, rows in enumerate(row_parts(half)):
            v_ref[t, rows, cols] = (
                g_ref[t, rows, cols] - uq_ref[0, t, rows, cols] * values[0][part]
            )

    norms = [jnp.zeros((8, 128), jnp.float32)] * 8

    def get_s(m, half):
        t, cols = time_at(m)
        return tuple(s_ref[t, rows, cols] for rows in row_parts(half))

    def put_s(m, half, values):
        t, cols = time_at(m)
        for part, rows in enumerate(row_parts(half)):
            g = v_ref[t, rows, cols] - values[0][part]
            g_ref[t, rows, cols] = g
            slot = 2 * (m % 4) + part
            norms[slot] = norms[slot] + g * g

    symbol = time_symbol(scale_ref[0], small_ref)
    transform(get_v, put_v, 1, symbol, dft_ref, small_ref, a_ref, b_ref, TIME_GROUP)
    transform(get_s, put_s, 1, symbol, dft_ref, small_ref, a_ref, b_ref, TIME_GROUP)
    copies.append(pltpu.make_async_copy(g_ref, out_ref.at[:, 32:64, :], sems.at[1]))
    copies[-1].start()
    cost = sum(costs) + 0.5 * p_cost_ref[...]
    norm = sum(norms)
    for m in range(16):
        sums_ref[m, :, 0:128] = cost
        sums_ref[m, :, 128:256] = norm
    copies.append(pltpu.make_async_copy(sums_ref, out_ref.at[:, 64:72, :], sems.at[2]))
    copies[-1].start()
    for copy in copies:
        copy.wait()


def sums_kernel(recv_ref, out_ref):
    total = jnp.sum(recv_ref[...], axis=0)
    cost = jnp.sum(total[:, 0:128], axis=0, keepdims=True)
    norm = jnp.sum(total[:, 128:256], axis=0, keepdims=True)
    row = lax.broadcasted_iota(jnp.int32, (8, 128), 0)
    out_ref[...] = jnp.broadcast_to(jnp.where(row == 0, cost, norm)[None], (8, 8, 128))


def unturn(recv_ref, first, ref):
    for h in range(2):
        for a in range(4):
            rows = slice(first + 8 * a, first + 8 * a + 8)
            tile = recv_ref[:, rows, h * 128 : h * 128 + 128]
            ref[h * 128 : h * 128 + 128, a * 128 : a * 128 + 128] = tile.reshape(128, 128).T


def unturn_kernel(recv_ref, q_ref, g_ref):
    unturn(recv_ref, 0, q_ref)
    unturn(recv_ref, 32, g_ref)


def residual_kernel(place_ref, q_ref, *refs):
    r_ref = refs[8]
    for d in range(8):
        rows = pl.ds(pl.multiple_of((place_ref[0] + 8 - d) % 8 * 32, 32), 32)
        r_ref[rows, :] = q_ref[rows, :] + refs[d][...]


def update_kernel(u_ref, g_ref, sums_ref, out_ref):
    sums = jnp.sum(sums_ref[...], axis=0)
    cost = jnp.sum(sums[0:1, :], axis=1, keepdims=True)
    norm = jnp.sum(sums[1:2, :], axis=1, keepdims=True)
    out_ref[...] = u_ref[...] - (cost / (norm + GRAD_EPS)) * g_ref[...]


VM = pl.BlockSpec(memory_space=pltpu.VMEM)
SM = pl.BlockSpec(memory_space=pltpu.SMEM)
HB = pl.BlockSpec(memory_space=pl.ANY)


def f32(*shape):
    return jax.ShapeDtypeStruct(shape, jnp.float32)


def call(kernel, outs, ins, scratch=(), sems=(), flops=0):
    return pl.pallas_call(
        kernel,
        out_shape=[f32(*shape) for shape, _ in outs],
        in_specs=[spec for _, spec in ins],
        out_specs=[spec for _, spec in outs],
        scratch_shapes=[pltpu.VMEM(shape, jnp.float32) for shape in scratch]
        + [pltpu.SemaphoreType.DMA((count,)) for count in sems],
        cost_estimate=pl.CostEstimate(flops=flops, bytes_accessed=2**21, transcendentals=0),
        compiler_params=pltpu.CompilerParams(vmem_limit_bytes=VMEM_LIMIT),
    )(*[array for array, _ in ins])


def shift_pairs(axis, shift):
    pairs = []
    for y in range(4):
        for x in range(4):
            to = (y, (x + shift) % 4) if axis else ((y + shift) % 4, x)
            pairs.append((4 * y + x, 4 * to[0] + to[1]))
    return pairs


def along_x(turned, x):
    pieces = turned.reshape(4, 4, 32, 256)
    moved = []
    for d in range(4):
        piece = lax.dynamic_index_in_dim(pieces, (x + d) % 4, 1, keepdims=False)
        moved.append(lax.ppermute(piece, "ta", shift_pairs(1, d)) if d else piece)
    return moved


def along_y(pieces, y):
    moved = []
    for e in range(4):
        piece = jnp.stack(
            [lax.dynamic_index_in_dim(part, (y + e) % 4, 0, keepdims=False) for part in pieces]
        )
        moved.append(lax.ppermute(piece, "ta", shift_pairs(0, e)) if e else piece)
    return jnp.stack(moved)


def local(field, time_period, space_period):
    dft_np, small_np = np_tables()
    dft = (jnp.asarray(dft_np), VM)
    small = (jnp.asarray(small_np), VM)
    time_scale = (TWO_PI / time_period, SM)
    space_scale = (TWO_PI / space_period, SM)
    rows, cols = (8, 32, 512), (16, 32, 256)
    planes = (RADIX, 16, 2 * SUB)
    here = lax.axis_index("ta")
    y, x = here // 4, here % 4
    z = lax.axis_index("gx")
    z_place = (z.reshape(1), SM)
    t_place = (jnp.stack([y, x]), SM)

    rows_u = lax.all_to_all(field.reshape(rows), "gx", 0, 0)
    (turned,) = call(turn_kernel, [(cols, VM)], [(field, VM)])
    first_move = along_x(turned, x)
    pieces, *p_planes, p_cost = call(
        space_kernel,
        [((8, 16, 16, 128), HB)] + [((32, 512), HB)] * 8 + [((8, 128), VM)],
        [space_scale, z_place, (rows_u, VM), dft, small],
        [rows, rows, (8, 16, 16, 128), planes, (2, *planes)],
        [8, 8],
        flops=8 * 10**9,
    )
    pieces, first_move = lax.optimization_barrier((pieces, first_move))
    received = lax.all_to_all(pieces.reshape(128, 16, 128), ("gx", "ta"), 0, 0)
    moved = along_y(first_move, y)
    (cols_uq,) = call(
        time_first_kernel,
        [((2, *cols), VM)],
        [time_scale, t_place, (moved, VM), dft, small],
        [planes, (1, *planes)],
        flops=2 * 10**9,
    )
    (cols_out,) = call(
        time_second_kernel,
        [((16, 72, 256), HB)],
        [time_scale, (cols_uq, VM), (received, VM), (p_cost, VM), dft, small],
        [cols, cols, cols, (16, 8, 256), planes, (1, *planes)],
        [3],
        flops=4 * 10**9,
    )
    cols_out, p_planes = lax.optimization_barrier((cols_out, p_planes))
    back = lax.all_to_all(cols_out, "ta", 0, 0)
    p_block = [
        lax.ppermute(plane, "gx", [(i, (i + d) % 8) for i in range(8)]) if d else plane
        for d, plane in enumerate(p_planes)
    ]
    (sums,) = call(sums_kernel, [((8, 8, 128), VM)], [(back[:, 64:72, :], VM)])
    sums = lax.all_to_all(sums, "gx", 0, 0)
    block_q, block_g = call(unturn_kernel, [((256, 512), VM), ((256, 512), VM)], [(back, VM)])
    (residual,) = call(
        residual_kernel,
        [((256, 512), VM)],
        [z_place, (block_q, VM)] + [(plane, VM) for plane in p_block],
    )
    (updated,) = call(
        update_kernel, [((256, 512), VM)], [(field, VM), (block_g, VM), (sums, VM)]
    )
    return updated, residual


def solution(mesh):
    placed = (P(("tile", "ta"), "gx"), P("tile"), P("tile"))
    return jax.shard_map(
        local,
        mesh=mesh,
        in_specs=placed,
        out_specs=(P(("tile", "ta"), "gx"), P(("tile", "ta"), "gx")),
        check_vma=False,
    )
```

```python
import math

import jax
import jax.numpy as jnp
import ml_dtypes
import numpy as np
from jax import lax
from jax.experimental import pallas as pl
from jax.experimental.pallas import tpu as pltpu
from jax.sharding import PartitionSpec as P

TWO_PI = 2.0 * math.pi
GRAD_EPS = 1e-06
LEN = 4096
RADIX = 32
SUB = 128
PARTS = 3
SPACE_GROUP = 16
TIME_GROUP = 8
VMEM_LIMIT = 24 * 1024 * 1024


def np_parts(values):
    rest = np.asarray(values, np.float64)
    parts = []
    for _ in range(PARTS):
        part = rest.astype(np.float32).astype(ml_dtypes.bfloat16)
        parts.append(part)
        rest = rest - part.astype(np.float64)
    return parts


def np_tables():
    j = np.arange(SUB)
    angle = TWO_PI * (np.outer(j, j) % SUB) / SUB
    cos, sin = np.cos(angle), np.sin(angle)
    dft = np.stack(np_parts(np.block([[cos, -sin], [sin, cos]])))
    k1 = np.arange(RADIX)
    twist = TWO_PI * np.outer(k1, j) / LEN
    mode = k1[:, None] + RADIX * j[None, :]
    signed = np.where(mode < LEN // 2, mode, mode - LEN)
    odd = np.where(mode == LEN // 2, 0, signed)
    small = np.stack([np.cos(twist), np.sin(twist), signed, odd]).astype(np.float32)
    return dft, small


def cadd(a, b):
    return (a[0] + b[0], a[1] + b[1])


def csub(a, b):
    return (a[0] - b[0], a[1] - b[1])


def dft4(x, sign):
    s = cadd(x[0], x[2])
    d = csub(x[0], x[2])
    t = cadd(x[1], x[3])
    e = csub(x[1], x[3])
    if sign < 0:
        ie = (e[1], -e[0])
    else:
        ie = (-e[1], e[0])
    return [cadd(s, t), cadd(d, ie), csub(s, t), csub(d, ie)]


def crot(x, turns, sign):
    turns = turns % 32
    if turns == 0:
        return x
    if turns == 8:
        return (x[1], -x[0]) if sign < 0 else (-x[1], x[0])
    c = math.cos(TWO_PI * turns / 32)
    s = sign * math.sin(TWO_PI * turns / 32)
    if turns == 4:
        return ((x[0] - sign * x[1]) * c, (x[1] + sign * x[0]) * c)
    if turns == 12:
        return ((x[0] + sign * x[1]) * c, (x[1] - sign * x[0]) * c)
    return (x[0] * c - x[1] * s, x[0] * s + x[1] * c)


def dft8(x, sign):
    even = dft4(x[0::2], sign)
    odd = [crot(value, 4 * k, sign) for k, value in enumerate(dft4(x[1::2], sign))]
    return [cadd(even[k], odd[k]) for k in range(4)] + [csub(even[k], odd[k]) for k in range(4)]


def dft32(x, sign):
    out = [None] * 32
    rows = []
    for n2 in range(8):
        y = dft4([x(8 * n1 + n2) for n1 in range(4)], sign)
        rows.append([crot(y[k1], n2 * k1, sign) for k1 in range(4)])
    for k1 in range(4):
        z = dft8([rows[n2][k1] for n2 in range(8)], sign)
        for k2 in range(8):
            out[k1 + 4 * k2] = z[k2]
    return out


def product(values, table_ref):
    parts = []
    rest = values
    for step in range(PARTS):
        part = rest.astype(jnp.bfloat16)
        parts.append(part)
        if step < PARTS - 1:
            rest = rest - part.astype(jnp.float32)
    order = [(i, k - i) for k in reversed(range(PARTS)) for i in range(k + 1)]
    left = jnp.concatenate([parts[i] for i, _ in order], axis=1)
    right = jnp.concatenate([table_ref[j] for _, j in order], axis=0)
    return jnp.dot(left, right, preferred_element_type=jnp.float32)


def transform(get, put, outputs, symbol, dft_ref, small_ref, a_ref, b_ref, group, after=None):
    re_lanes, im_lanes = slice(0, SUB), slice(SUB, 2 * SUB)
    for half in range(2):
        rows = slice(8 * half, 8 * half + 8)
        planes = dft32(lambda m: get(m, half), -1)
        for k1 in range(RADIX):
            re, im = planes[k1]
            if k1:
                c = small_ref[0, k1 : k1 + 1, :]
                s = small_ref[1, k1 : k1 + 1, :]
                re, im = re * c + im * s, im * c - re * s
            a_ref[k1, rows, re_lanes] = re
            a_ref[k1, rows, im_lanes] = im
    for first in range(0, RADIX, group):
        ks = slice(first, first + group)
        got = product(a_ref[ks].reshape(group * 16, 2 * SUB), dft_ref)
        got = got.reshape(group, 16, 2 * SUB)
        re, im = got[:, :, re_lanes], got[:, :, im_lanes]
        swapped = [
            jnp.concatenate(symbol(o, ks, re, im)[::-1], axis=2).reshape(group * 16, 2 * SUB)
            for o in range(outputs)
        ]
        got = product(jnp.concatenate(swapped, axis=0), dft_ref)
        got = got.reshape(outputs, group, 16, 2 * SUB)
        c = small_ref[0, ks][:, None, :]
        s = small_ref[1, ks][:, None, :]
        for o in range(outputs):
            im2, re2 = got[o, :, :, re_lanes], got[o, :, :, im_lanes]
            b_ref[o, ks, :, re_lanes] = re2 * c - im2 * s
            b_ref[o, ks, :, im_lanes] = im2 * c + re2 * s
    for half in range(2):
        rows = slice(8 * half, 8 * half + 8)
        outs = [
            dft32(lambda k: (b_ref[o, k, rows, re_lanes], b_ref[o, k, rows, im_lanes]), 1)
            for o in range(outputs)
        ]
        for m in range(RADIX):
            put(m, half, [outs[o][m] for o in range(outputs)])
        if after is not None:
            after(half)


def space_symbol(scale, small_ref):
    def symbol(o, ks, re, im):
        if o == 0:
            wave = small_ref[2, ks] * scale
            square = wave * wave
            even = ((square * square - square) * (1.0 / LEN))[:, None, :]
            return re * even, im * even
        odd = (small_ref[3, ks] * (scale * (1.0 / LEN)))[:, None, :]
        return -im * odd, re * odd

    return symbol


def time_symbol(scale, small_ref):
    def symbol(o, ks, re, im):
        odd = (small_ref[3, ks] * (scale * (1.0 / LEN)))[:, None, :]
        return -im * odd, re * odd

    return symbol


def row_parts(half):
    return slice(8 * half, 8 * half + 8), slice(16 + 8 * half, 24 + 8 * half)


def space_at(m):
    return m // 4, slice((m % 4) * 128, (m % 4) * 128 + 128)


def time_at(m):
    return m // 2, slice((m % 2) * 128, (m % 2) * 128 + 128)


def blocks4(tiles):
    lane = lax.broadcasted_iota(jnp.int32, tiles[0].shape, len(tiles[0].shape) - 1)
    axis = len(tiles[0].shape) - 1
    low_half = lane < 64
    even = (lane // 32) % 2 == 0

    def swap(x, y, shift, mask):
        first = jnp.where(mask, x, pltpu.roll(y, shift, axis))
        second = jnp.where(mask, pltpu.roll(x, 128 - shift, axis), y)
        return first, second

    t0, t2 = swap(tiles[0], tiles[2], 64, low_half)
    t1, t3 = swap(tiles[1], tiles[3], 64, low_half)
    t0, t1 = swap(t0, t1, 32, even)
    t2, t3 = swap(t2, t3, 32, even)
    return [t0, t1, t2, t3]


def turn_kernel(u_ref, out_ref):
    for h in range(2):
        for a in range(4):
            tile = u_ref[h * 128 : h * 128 + 128, a * 128 : a * 128 + 128].T
            out_ref[:, a * 8 : a * 8 + 8, h * 128 : h * 128 + 128] = tile.reshape(16, 8, 128)


def fold(values):
    lanes = sum(values[:, a * 128 : a * 128 + 128] for a in range(4))
    return sum(lanes[8 * a : 8 * a + 8] for a in range(4))


def space_kernel(
    scale_ref,
    place_ref,
    u_ref,
    dft_ref,
    small_ref,
    out_ref,
    *rest,
):
    p_outs = rest[:8]
    cost_ref, p_ref, v_ref, send_ref, a_ref, b_ref, sems, p_sems = rest[8:]

    def pack(ref, g, slot):
        stack = jnp.concatenate([ref[g, :, a * 128 : a * 128 + 128] for a in range(4)], axis=0)
        send_ref[g, :, 8 * slot : 8 * slot + 8, :] = stack.T.reshape(16, 8, 128)

    def get_u(m, half):
        g, cols = space_at(m)
        return tuple(u_ref[g, rows, cols] for rows in row_parts(half))

    def put_u(m, half, values):
        g, cols = space_at(m)
        for part, rows in enumerate(row_parts(half)):
            p = values[0][part] + u_ref[g, rows, cols] * values[1][part]
            p_ref[g, rows, cols] = p
            v_ref[g, rows, cols] = values[1][part]

    def get_p(m, half):
        g, cols = space_at(m)
        return tuple(p_ref[g, rows, cols] for rows in row_parts(half))

    def put_p(m, half, values):
        g, cols = space_at(m)
        for part, rows in enumerate(row_parts(half)):
            v_ref[g, rows, cols] = values[0][part] - u_ref[g, rows, cols] * values[1][part]

    symbol = space_symbol(scale_ref[0], small_ref)
    transform(get_u, put_u, 2, symbol, dft_ref, small_ref, a_ref, b_ref, SPACE_GROUP)
    copies = []
    for d in range(8):
        plane = (place_ref[0] + d) % 8
        copies.append(pltpu.make_async_copy(p_ref.at[plane], p_outs[d], p_sems.at[d]))
        copies[-1].start()
    cost_ref[...] = fold(jnp.sum(p_ref[...] * p_ref[...], axis=0))
    for g in range(8):
        pack(v_ref, g, 0)
    transform(get_p, put_p, 2, symbol, dft_ref, small_ref, a_ref, b_ref, SPACE_GROUP)
    for g in range(8):
        pack(v_ref, g, 1)
        copies.append(pltpu.make_async_copy(send_ref.at[g], out_ref.at[g], sems.at[g]))
        copies[-1].start()
    for copy in copies:
        copy.wait()


def time_first_kernel(scale_ref, place_ref, moved_ref, dft_ref, small_ref, uq_ref, a_ref, b_ref):
    for m in range(16):
        uq_ref[0, m] = moved_ref[(place_ref[0] + 4 - m // 4) % 4, (place_ref[1] + 4 - m % 4) % 4]

    def get(m, half):
        t, cols = time_at(m)
        return tuple(uq_ref[0, t, rows, cols] for rows in row_parts(half))

    def put(m, half, values):
        t, cols = time_at(m)
        for part, rows in enumerate(row_parts(half)):
            uq_ref[1, t, rows, cols] = values[0][part]

    symbol = time_symbol(scale_ref[0], small_ref)
    transform(get, put, 1, symbol, dft_ref, small_ref, a_ref, b_ref, TIME_GROUP)


def time_second_kernel(
    scale_ref,
    uq_ref,
    recv_ref,
    p_cost_ref,
    dft_ref,
    small_ref,
    out_ref,
    v_ref,
    s_ref,
    g_ref,
    sums_ref,
    a_ref,
    b_ref,
    sems,
):
    copies = []

    def send(ref, first, sem):
        for h in range(2):
            lanes = slice(h * 128, h * 128 + 128)
            rows = slice(first + 32 * h, first + 32 * h + 32)
            copies.append(
                pltpu.make_async_copy(ref.at[:, :, lanes], out_ref.at[:, rows, :], sems.at[sem + h])
            )
            copies[-1].start()

    send(uq_ref.at[1], 0, 0)
    costs = [jnp.zeros((8, 128), jnp.float32)] * 8
    for m in range(16):
        for h in range(2):
            cols = slice(h * 128, h * 128 + 128)
            for o, ref in enumerate((v_ref, g_ref)):
                tiles = blocks4([recv_ref[(4 * h + k) * 16 + m, 8 * o : 8 * o + 8] for k in range(4)])
                for a in range(4):
                    rows = slice(8 * a, 8 * a + 8)
                    ref[m, rows, cols] = tiles[a]
                    if o == 0:
                        q = uq_ref[1, m, rows, cols]
                        w = uq_ref[0, m, rows, cols] * tiles[a]
                        s_ref[m, rows, cols] = q + w
                        costs[4 * h + a] = costs[4 * h + a] + q * (0.5 * q + w)

    def get_v(m, half):
        t, cols = time_at(m)
        return tuple(v_ref[t, rows, cols] for rows in row_parts(half))

    def put_v(m, half, values):
        t, cols = time_at(m)
        for part, rows in enumerate(row_parts(half)):
            v_ref[t, rows, cols] = (
                g_ref[t, rows, cols] - uq_ref[0, t, rows, cols] * values[0][part]
            )

    norms = [jnp.zeros((8, 128), jnp.float32)] * 8

    def get_s(m, half):
        t, cols = time_at(m)
        return tuple(s_ref[t, rows, cols] for rows in row_parts(half))

    def put_s(m, half, values):
        t, cols = time_at(m)
        for part, rows in enumerate(row_parts(half)):
            g = v_ref[t, rows, cols] - values[0][part]
            g_ref[t, rows, cols] = g
            slot = 2 * (m % 4) + part
            norms[slot] = norms[slot] + g * g

    symbol = time_symbol(scale_ref[0], small_ref)
    transform(get_v, put_v, 1, symbol, dft_ref, small_ref, a_ref, b_ref, TIME_GROUP)
    transform(get_s, put_s, 1, symbol, dft_ref, small_ref, a_ref, b_ref, TIME_GROUP)
    send(g_ref, 64, 2)
    cost = sum(costs) + 0.5 * p_cost_ref[...]
    norm = sum(norms)
    both = jnp.concatenate([cost[0:4] + cost[4:8], norm[0:4] + norm[4:8]], axis=0)
    sums_ref[...] = jnp.broadcast_to(both[None], (16, 8, 128))
    copies.append(pltpu.make_async_copy(sums_ref, out_ref.at[:, 128:136, :], sems.at[4]))
    copies[-1].start()
    for copy in copies:
        copy.wait()


def sums_kernel(recv_ref, out_ref):
    total = jnp.sum(recv_ref[...], axis=0)
    cost = jnp.sum(total[0:4], axis=0, keepdims=True)
    norm = jnp.sum(total[4:8], axis=0, keepdims=True)
    row = lax.broadcasted_iota(jnp.int32, (8, 128), 0)
    out_ref[...] = jnp.broadcast_to(jnp.where(row == 0, cost, norm)[None], (8, 8, 128))


def unturn(recv_ref, first, ref):
    for h in range(2):
        for a in range(4):
            rows = slice(first + 32 * h + 8 * a, first + 32 * h + 8 * a + 8)
            tile = recv_ref[:, rows, :]
            ref[h * 128 : h * 128 + 128, a * 128 : a * 128 + 128] = tile.reshape(128, 128).T


def unturn_kernel(recv_ref, q_ref, g_ref):
    unturn(recv_ref, 0, q_ref)
    unturn(recv_ref, 64, g_ref)


def residual_kernel(place_ref, q_ref, *refs):
    r_ref = refs[8]
    for d in range(8):
        rows = pl.ds(pl.multiple_of((place_ref[0] + 8 - d) % 8 * 32, 32), 32)
        r_ref[rows, :] = q_ref[rows, :] + refs[d][...]


def update_kernel(u_ref, g_ref, sums_ref, out_ref):
    sums = jnp.sum(sums_ref[...], axis=0)
    cost = jnp.sum(sums[0:1, :], axis=1, keepdims=True)
    norm = jnp.sum(sums[1:2, :], axis=1, keepdims=True)
    out_ref[...] = u_ref[...] - (cost / (norm + GRAD_EPS)) * g_ref[...]


VM = pl.BlockSpec(memory_space=pltpu.VMEM)
SM = pl.BlockSpec(memory_space=pltpu.SMEM)
HB = pl.BlockSpec(memory_space=pl.ANY)


def f32(*shape):
    return jax.ShapeDtypeStruct(shape, jnp.float32)


def call(kernel, outs, ins, scratch=(), sems=(), flops=0):
    return pl.pallas_call(
        kernel,
        out_shape=[f32(*shape) for shape, _ in outs],
        in_specs=[spec for _, spec in ins],
        out_specs=[spec for _, spec in outs],
        scratch_shapes=[pltpu.VMEM(shape, jnp.float32) for shape in scratch]
        + [pltpu.SemaphoreType.DMA((count,)) for count in sems],
        cost_estimate=pl.CostEstimate(flops=flops, bytes_accessed=2**21, transcendentals=0),
        compiler_params=pltpu.CompilerParams(vmem_limit_bytes=VMEM_LIMIT),
    )(*[array for array, _ in ins])


def shift_pairs(axis, shift):
    pairs = []
    for y in range(4):
        for x in range(4):
            to = (y, (x + shift) % 4) if axis else ((y + shift) % 4, x)
            pairs.append((4 * y + x, 4 * to[0] + to[1]))
    return pairs


def along_x(turned, x):
    pieces = turned.reshape(4, 4, 32, 256)
    moved = []
    for d in range(4):
        piece = lax.dynamic_index_in_dim(pieces, (x + d) % 4, 1, keepdims=False)
        moved.append(lax.ppermute(piece, "ta", shift_pairs(1, d)) if d else piece)
    return moved


def along_y(pieces, y):
    moved = []
    for e in range(4):
        piece = jnp.stack(
            [lax.dynamic_index_in_dim(part, (y + e) % 4, 0, keepdims=False) for part in pieces]
        )
        moved.append(lax.ppermute(piece, "ta", shift_pairs(0, e)) if e else piece)
    return jnp.stack(moved)


def local(field, time_period, space_period):
    dft_np, small_np = np_tables()
    dft = (jnp.asarray(dft_np), VM)
    small = (jnp.asarray(small_np), VM)
    time_scale = (TWO_PI / time_period, SM)
    space_scale = (TWO_PI / space_period, SM)
    rows, cols = (8, 32, 512), (16, 32, 256)
    planes = (RADIX, 16, 2 * SUB)
    here = lax.axis_index("ta")
    y, x = here // 4, here % 4
    z = lax.axis_index("gx")
    z_place = (z.reshape(1), SM)
    t_place = (jnp.stack([y, x]), SM)

    rows_u = lax.all_to_all(field.reshape(rows), "gx", 0, 0)
    (turned,) = call(turn_kernel, [(cols, VM)], [(field, VM)])
    first_move = along_x(turned, x)
    pieces, *p_planes, p_cost = call(
        space_kernel,
        [((8, 16, 16, 128), HB)] + [((32, 512), HB)] * 8 + [((8, 128), VM)],
        [space_scale, z_place, (rows_u, VM), dft, small],
        [rows, rows, (8, 16, 16, 128), planes, (2, *planes)],
        [8, 8],
        flops=8 * 10**9,
    )
    pieces, first_move = lax.optimization_barrier((pieces, first_move))
    received = lax.all_to_all(pieces.reshape(128, 16, 128), ("gx", "ta"), 0, 0)
    moved = along_y(first_move, y)
    (cols_uq,) = call(
        time_first_kernel,
        [((2, *cols), VM)],
        [time_scale, t_place, (moved, VM), dft, small],
        [planes, (1, *planes)],
        flops=2 * 10**9,
    )
    (cols_out,) = call(
        time_second_kernel,
        [((16, 136, 128), HB)],
        [time_scale, (cols_uq, VM), (received, VM), (p_cost, VM), dft, small],
        [cols, cols, cols, (16, 8, 128), planes, (1, *planes)],
        [5],
        flops=4 * 10**9,
    )
    cols_out, p_planes = lax.optimization_barrier((cols_out, p_planes))
    back = lax.all_to_all(cols_out, "ta", 0, 0)
    p_block = [
        lax.ppermute(plane, "gx", [(i, (i + d) % 8) for i in range(8)]) if d else plane
        for d, plane in enumerate(p_planes)
    ]
    (sums,) = call(sums_kernel, [((8, 8, 128), VM)], [(back[:, 128:136, :], VM)])
    sums = lax.all_to_all(sums, "gx", 0, 0)
    block_q, block_g = call(unturn_kernel, [((256, 512), VM), ((256, 512), VM)], [(back, VM)])
    (residual,) = call(
        residual_kernel,
        [((256, 512), VM)],
        [z_place, (block_q, VM)] + [(plane, VM) for plane in p_block],
    )
    (updated,) = call(
        update_kernel, [((256, 512), VM)], [(field, VM), (block_g, VM), (sums, VM)]
    )
    return updated, residual


def solution(mesh):
    placed = (P(("tile", "ta"), "gx"), P("tile"), P("tile"))
    return jax.shard_map(
        local,
        mesh=mesh,
        in_specs=placed,
        out_specs=(P(("tile", "ta"), "gx"), P(("tile", "ta"), "gx")),
        check_vma=False,
    )
```

```python
import math

import jax
import jax.numpy as jnp
import ml_dtypes
import numpy as np
from jax import lax
from jax.experimental import pallas as pl
from jax.experimental.pallas import tpu as pltpu
from jax.sharding import PartitionSpec as P

TWO_PI = 2.0 * math.pi
GRAD_EPS = 1e-06
LEN = 4096
RADIX = 32
SUB = 128
PARTS = 3
SPACE_GROUP = 32
TIME_GROUP = 16
VMEM_LIMIT = 24 * 1024 * 1024


def np_parts(values):
    rest = np.asarray(values, np.float64)
    parts = []
    for _ in range(PARTS):
        part = rest.astype(np.float32).astype(ml_dtypes.bfloat16)
        parts.append(part)
        rest = rest - part.astype(np.float64)
    return parts


def np_tables():
    j = np.arange(SUB)
    angle = TWO_PI * (np.outer(j, j) % SUB) / SUB
    cos, sin = np.cos(angle), np.sin(angle)
    dft = np.stack(np_parts(np.block([[cos, -sin], [sin, cos]])))
    k1 = np.arange(RADIX)
    twist = TWO_PI * np.outer(k1, j) / LEN
    mode = k1[:, None] + RADIX * j[None, :]
    signed = np.where(mode < LEN // 2, mode, mode - LEN)
    odd = np.where(mode == LEN // 2, 0, signed)
    small = np.stack([np.cos(twist), np.sin(twist), signed, odd]).astype(np.float32)
    return dft, small


def cadd(a, b):
    return (a[0] + b[0], a[1] + b[1])


def csub(a, b):
    return (a[0] - b[0], a[1] - b[1])


def dft4(x, sign):
    s = cadd(x[0], x[2])
    d = csub(x[0], x[2])
    t = cadd(x[1], x[3])
    e = csub(x[1], x[3])
    if sign < 0:
        ie = (e[1], -e[0])
    else:
        ie = (-e[1], e[0])
    return [cadd(s, t), cadd(d, ie), csub(s, t), csub(d, ie)]


def crot(x, turns, sign):
    turns = turns % 32
    if turns == 0:
        return x
    if turns == 8:
        return (x[1], -x[0]) if sign < 0 else (-x[1], x[0])
    c = math.cos(TWO_PI * turns / 32)
    s = sign * math.sin(TWO_PI * turns / 32)
    if turns == 4:
        return ((x[0] - sign * x[1]) * c, (x[1] + sign * x[0]) * c)
    if turns == 12:
        return ((x[0] + sign * x[1]) * c, (x[1] - sign * x[0]) * c)
    return (x[0] * c - x[1] * s, x[0] * s + x[1] * c)


def dft8(x, sign):
    even = dft4(x[0::2], sign)
    odd = [crot(value, 4 * k, sign) for k, value in enumerate(dft4(x[1::2], sign))]
    return [cadd(even[k], odd[k]) for k in range(4)] + [csub(even[k], odd[k]) for k in range(4)]


def dft32(x, sign):
    out = [None] * 32
    rows = []
    for n2 in range(8):
        y = dft4([x(8 * n1 + n2) for n1 in range(4)], sign)
        rows.append([crot(y[k1], n2 * k1, sign) for k1 in range(4)])
    for k1 in range(4):
        z = dft8([rows[n2][k1] for n2 in range(8)], sign)
        for k2 in range(8):
            out[k1 + 4 * k2] = z[k2]
    return out


def product(values, table_ref):
    parts = []
    rest = values
    for step in range(PARTS):
        part = rest.astype(jnp.bfloat16)
        parts.append(part)
        if step < PARTS - 1:
            rest = rest - part.astype(jnp.float32)
    order = [(i, k - i) for k in reversed(range(PARTS)) for i in range(k + 1)]
    left = jnp.concatenate([parts[i] for i, _ in order], axis=1)
    right = jnp.concatenate([table_ref[j] for _, j in order], axis=0)
    return jnp.dot(left, right, preferred_element_type=jnp.float32)


def transform(get, put, outputs, symbol, dft_ref, small_ref, a_ref, b_ref, group):
    re_lanes, im_lanes = slice(0, SUB), slice(SUB, 2 * SUB)

    def forward(half):
        rows = slice(8 * half, 8 * half + 8)
        planes = dft32(lambda m: get(m, half), -1)
        for k1 in range(RADIX):
            re, im = planes[k1]
            if k1:
                c = small_ref[0, k1 : k1 + 1, :]
                s = small_ref[1, k1 : k1 + 1, :]
                re, im = re * c + im * s, im * c - re * s
            a_ref[k1, rows, re_lanes] = re
            a_ref[k1, rows, im_lanes] = im

    def middle(half):
        rows = slice(8 * half, 8 * half + 8)
        for first in range(0, RADIX, group):
            ks = slice(first, first + group)
            got = product(a_ref[ks, rows].reshape(group * 8, 2 * SUB), dft_ref)
            got = got.reshape(group, 8, 2 * SUB)
            re, im = got[:, :, re_lanes], got[:, :, im_lanes]
            swapped = [
                jnp.concatenate(symbol(o, ks, re, im)[::-1], axis=2).reshape(group * 8, 2 * SUB)
                for o in range(outputs)
            ]
            got = product(jnp.concatenate(swapped, axis=0), dft_ref)
            got = got.reshape(outputs, group, 8, 2 * SUB)
            c = small_ref[0, ks][:, None, :]
            s = small_ref[1, ks][:, None, :]
            for o in range(outputs):
                im2, re2 = got[o, :, :, re_lanes], got[o, :, :, im_lanes]
                b_ref[o, ks, rows, re_lanes] = re2 * c - im2 * s
                b_ref[o, ks, rows, im_lanes] = im2 * c + re2 * s

    def inverse(half):
        rows = slice(8 * half, 8 * half + 8)
        outs = [
            dft32(lambda k: (b_ref[o, k, rows, re_lanes], b_ref[o, k, rows, im_lanes]), 1)
            for o in range(outputs)
        ]
        for m in range(RADIX):
            put(m, half, [outs[o][m] for o in range(outputs)])

    forward(0)
    forward(1)
    middle(0)
    middle(1)
    inverse(0)
    inverse(1)


def space_symbol(scale, small_ref):
    def symbol(o, ks, re, im):
        if o == 0:
            wave = small_ref[2, ks] * scale
            square = wave * wave
            even = ((square * square - square) * (1.0 / LEN))[:, None, :]
            return re * even, im * even
        odd = (small_ref[3, ks] * (scale * (1.0 / LEN)))[:, None, :]
        return -im * odd, re * odd

    return symbol


def time_symbol(scale, small_ref):
    def symbol(o, ks, re, im):
        odd = (small_ref[3, ks] * (scale * (1.0 / LEN)))[:, None, :]
        return -im * odd, re * odd

    return symbol


def row_parts(half):
    return slice(8 * half, 8 * half + 8), slice(16 + 8 * half, 24 + 8 * half)


def space_at(m):
    return m // 4, slice((m % 4) * 128, (m % 4) * 128 + 128)


def time_at(m):
    return m // 2, slice((m % 2) * 128, (m % 2) * 128 + 128)


def blocks4(tiles):
    lane = lax.broadcasted_iota(jnp.int32, tiles[0].shape, len(tiles[0].shape) - 1)
    axis = len(tiles[0].shape) - 1
    low_half = lane < 64
    even = (lane // 32) % 2 == 0

    def swap(x, y, shift, mask):
        first = jnp.where(mask, x, pltpu.roll(y, shift, axis))
        second = jnp.where(mask, pltpu.roll(x, 128 - shift, axis), y)
        return first, second

    t0, t2 = swap(tiles[0], tiles[2], 64, low_half)
    t1, t3 = swap(tiles[1], tiles[3], 64, low_half)
    t0, t1 = swap(t0, t1, 32, even)
    t2, t3 = swap(t2, t3, 32, even)
    return [t0, t1, t2, t3]


def turn_kernel(u_ref, out_ref):
    for h in range(2):
        for a in range(4):
            tile = u_ref[h * 128 : h * 128 + 128, a * 128 : a * 128 + 128].T
            out_ref[:, a * 8 : a * 8 + 8, h * 128 : h * 128 + 128] = tile.reshape(16, 8, 128)


def fold(values):
    lanes = sum(values[:, a * 128 : a * 128 + 128] for a in range(4))
    return sum(lanes[8 * a : 8 * a + 8] for a in range(4))


def space_kernel(
    scale_ref,
    place_ref,
    u_ref,
    dft_ref,
    small_ref,
    out_ref,
    *rest,
):
    p_outs = rest[:8]
    cost_ref, p_ref, v_ref, send_ref, a_ref, b_ref, sems, p_sems = rest[8:]

    def pack(ref, g, slot):
        stack = jnp.concatenate([ref[g, :, a * 128 : a * 128 + 128] for a in range(4)], axis=0)
        send_ref[g, :, 8 * slot : 8 * slot + 8, :] = stack.T.reshape(16, 8, 128)

    def get_u(m, half):
        g, cols = space_at(m)
        return tuple(u_ref[g, rows, cols] for rows in row_parts(half))

    def put_u(m, half, values):
        g, cols = space_at(m)
        for part, rows in enumerate(row_parts(half)):
            p = values[0][part] + u_ref[g, rows, cols] * values[1][part]
            p_ref[g, rows, cols] = p
            v_ref[g, rows, cols] = values[1][part]

    def get_p(m, half):
        g, cols = space_at(m)
        return tuple(p_ref[g, rows, cols] for rows in row_parts(half))

    def put_p(m, half, values):
        g, cols = space_at(m)
        for part, rows in enumerate(row_parts(half)):
            v_ref[g, rows, cols] = values[0][part] - u_ref[g, rows, cols] * values[1][part]

    symbol = space_symbol(scale_ref[0], small_ref)
    transform(get_u, put_u, 2, symbol, dft_ref, small_ref, a_ref, b_ref, SPACE_GROUP)
    copies = []
    for d in range(8):
        plane = (place_ref[0] + d) % 8
        copies.append(pltpu.make_async_copy(p_ref.at[plane], p_outs[d], p_sems.at[d]))
        copies[-1].start()
    cost_ref[...] = fold(jnp.sum(p_ref[...] * p_ref[...], axis=0))
    for g in range(8):
        pack(v_ref, g, 0)
    transform(get_p, put_p, 2, symbol, dft_ref, small_ref, a_ref, b_ref, SPACE_GROUP)
    for g in range(8):
        pack(v_ref, g, 1)
        copies.append(pltpu.make_async_copy(send_ref.at[g], out_ref.at[g], sems.at[g]))
        copies[-1].start()
    for copy in copies:
        copy.wait()


def time_first_kernel(scale_ref, place_ref, moved_ref, dft_ref, small_ref, uq_ref, a_ref, b_ref):
    for m in range(16):
        uq_ref[0, m] = moved_ref[(place_ref[0] + 4 - m // 4) % 4, (place_ref[1] + 4 - m % 4) % 4]

    def get(m, half):
        t, cols = time_at(m)
        return tuple(uq_ref[0, t, rows, cols] for rows in row_parts(half))

    def put(m, half, values):
        t, cols = time_at(m)
        for part, rows in enumerate(row_parts(half)):
            uq_ref[1, t, rows, cols] = values[0][part]

    symbol = time_symbol(scale_ref[0], small_ref)
    transform(get, put, 1, symbol, dft_ref, small_ref, a_ref, b_ref, TIME_GROUP)


def time_second_kernel(
    scale_ref,
    uq_ref,
    recv_ref,
    p_cost_ref,
    dft_ref,
    small_ref,
    out_ref,
    v_ref,
    s_ref,
    g_ref,
    sums_ref,
    a_ref,
    b_ref,
    sems,
):
    copies = []

    def send(ref, first, sem):
        for h in range(2):
            lanes = slice(h * 128, h * 128 + 128)
            rows = slice(first + 32 * h, first + 32 * h + 32)
            copies.append(
                pltpu.make_async_copy(ref.at[:, :, lanes], out_ref.at[:, rows, :], sems.at[sem + h])
            )
            copies[-1].start()

    send(uq_ref.at[1], 0, 0)
    costs = [jnp.zeros((8, 128), jnp.float32)] * 8
    for m in range(16):
        for h in range(2):
            cols = slice(h * 128, h * 128 + 128)
            for o, ref in enumerate((v_ref, g_ref)):
                tiles = blocks4([recv_ref[(4 * h + k) * 16 + m, 8 * o : 8 * o + 8] for k in range(4)])
                for a in range(4):
                    rows = slice(8 * a, 8 * a + 8)
                    ref[m, rows, cols] = tiles[a]
                    if o == 0:
                        q = uq_ref[1, m, rows, cols]
                        w = uq_ref[0, m, rows, cols] * tiles[a]
                        s_ref[m, rows, cols] = q + w
                        costs[4 * h + a] = costs[4 * h + a] + q * (0.5 * q + w)

    def get_v(m, half):
        t, cols = time_at(m)
        return tuple(v_ref[t, rows, cols] for rows in row_parts(half))

    def put_v(m, half, values):
        t, cols = time_at(m)
        for part, rows in enumerate(row_parts(half)):
            v_ref[t, rows, cols] = (
                g_ref[t, rows, cols] - uq_ref[0, t, rows, cols] * values[0][part]
            )

    norms = [jnp.zeros((8, 128), jnp.float32)] * 8

    def get_s(m, half):
        t, cols = time_at(m)
        return tuple(s_ref[t, rows, cols] for rows in row_parts(half))

    def put_s(m, half, values):
        t, cols = time_at(m)
        for part, rows in enumerate(row_parts(half)):
            g = v_ref[t, rows, cols] - values[0][part]
            g_ref[t, rows, cols] = g
            slot = 2 * (m % 4) + part
            norms[slot] = norms[slot] + g * g

    symbol = time_symbol(scale_ref[0], small_ref)
    transform(get_v, put_v, 1, symbol, dft_ref, small_ref, a_ref, b_ref, TIME_GROUP)
    transform(get_s, put_s, 1, symbol, dft_ref, small_ref, a_ref, b_ref, TIME_GROUP)
    send(g_ref, 64, 2)
    cost = sum(costs) + 0.5 * p_cost_ref[...]
    norm = sum(norms)
    both = jnp.concatenate([cost[0:4] + cost[4:8], norm[0:4] + norm[4:8]], axis=0)
    sums_ref[...] = jnp.broadcast_to(both[None], (16, 8, 128))
    copies.append(pltpu.make_async_copy(sums_ref, out_ref.at[:, 128:136, :], sems.at[4]))
    copies[-1].start()
    for copy in copies:
        copy.wait()


def sums_kernel(recv_ref, out_ref):
    total = jnp.sum(recv_ref[...], axis=0)
    cost = jnp.sum(total[0:4], axis=0, keepdims=True)
    norm = jnp.sum(total[4:8], axis=0, keepdims=True)
    row = lax.broadcasted_iota(jnp.int32, (8, 128), 0)
    out_ref[...] = jnp.broadcast_to(jnp.where(row == 0, cost, norm)[None], (8, 8, 128))


def unturn(recv_ref, first, ref):
    for h in range(2):
        for a in range(4):
            rows = slice(first + 32 * h + 8 * a, first + 32 * h + 8 * a + 8)
            tile = recv_ref[:, rows, :]
            ref[h * 128 : h * 128 + 128, a * 128 : a * 128 + 128] = tile.reshape(128, 128).T


def unturn_kernel(recv_ref, q_ref, g_ref):
    unturn(recv_ref, 0, q_ref)
    unturn(recv_ref, 64, g_ref)


def residual_kernel(place_ref, q_ref, *refs):
    r_ref = refs[8]
    for d in range(8):
        rows = pl.ds(pl.multiple_of((place_ref[0] + 8 - d) % 8 * 32, 32), 32)
        r_ref[rows, :] = q_ref[rows, :] + refs[d][...]


def update_kernel(u_ref, g_ref, sums_ref, out_ref):
    sums = jnp.sum(sums_ref[...], axis=0)
    cost = jnp.sum(sums[0:1, :], axis=1, keepdims=True)
    norm = jnp.sum(sums[1:2, :], axis=1, keepdims=True)
    out_ref[...] = u_ref[...] - (cost / (norm + GRAD_EPS)) * g_ref[...]


VM = pl.BlockSpec(memory_space=pltpu.VMEM)
SM = pl.BlockSpec(memory_space=pltpu.SMEM)
HB = pl.BlockSpec(memory_space=pl.ANY)


def f32(*shape):
    return jax.ShapeDtypeStruct(shape, jnp.float32)


def call(kernel, outs, ins, scratch=(), sems=(), flops=0):
    return pl.pallas_call(
        kernel,
        out_shape=[f32(*shape) for shape, _ in outs],
        in_specs=[spec for _, spec in ins],
        out_specs=[spec for _, spec in outs],
        scratch_shapes=[pltpu.VMEM(shape, jnp.float32) for shape in scratch]
        + [pltpu.SemaphoreType.DMA((count,)) for count in sems],
        cost_estimate=pl.CostEstimate(flops=flops, bytes_accessed=2**21, transcendentals=0),
        compiler_params=pltpu.CompilerParams(vmem_limit_bytes=VMEM_LIMIT),
    )(*[array for array, _ in ins])


def shift_pairs(axis, shift):
    pairs = []
    for y in range(4):
        for x in range(4):
            to = (y, (x + shift) % 4) if axis else ((y + shift) % 4, x)
            pairs.append((4 * y + x, 4 * to[0] + to[1]))
    return pairs


def along_x(turned, x):
    pieces = turned.reshape(4, 4, 32, 256)
    moved = []
    for d in range(4):
        piece = lax.dynamic_index_in_dim(pieces, (x + d) % 4, 1, keepdims=False)
        moved.append(lax.ppermute(piece, "ta", shift_pairs(1, d)) if d else piece)
    return moved


def along_y(pieces, y):
    moved = []
    for e in range(4):
        piece = jnp.stack(
            [lax.dynamic_index_in_dim(part, (y + e) % 4, 0, keepdims=False) for part in pieces]
        )
        moved.append(lax.ppermute(piece, "ta", shift_pairs(0, e)) if e else piece)
    return jnp.stack(moved)


def local(field, time_period, space_period):
    dft_np, small_np = np_tables()
    dft = (jnp.asarray(dft_np), VM)
    small = (jnp.asarray(small_np), VM)
    time_scale = (TWO_PI / time_period, SM)
    space_scale = (TWO_PI / space_period, SM)
    rows, cols = (8, 32, 512), (16, 32, 256)
    planes = (RADIX, 16, 2 * SUB)
    here = lax.axis_index("ta")
    y, x = here // 4, here % 4
    z = lax.axis_index("gx")
    z_place = (z.reshape(1), SM)
    t_place = (jnp.stack([y, x]), SM)

    rows_u = lax.all_to_all(field.reshape(rows), "gx", 0, 0)
    (turned,) = call(turn_kernel, [(cols, VM)], [(field, VM)])
    first_move = along_x(turned, x)
    pieces, *p_planes, p_cost = call(
        space_kernel,
        [((8, 16, 16, 128), HB)] + [((32, 512), HB)] * 8 + [((8, 128), VM)],
        [space_scale, z_place, (rows_u, VM), dft, small],
        [rows, rows, (8, 16, 16, 128), planes, (2, *planes)],
        [8, 8],
        flops=8 * 10**9,
    )
    pieces, first_move = lax.optimization_barrier((pieces, first_move))
    received = lax.all_to_all(pieces.reshape(128, 16, 128), ("gx", "ta"), 0, 0)
    moved = along_y(first_move, y)
    (cols_uq,) = call(
        time_first_kernel,
        [((2, *cols), VM)],
        [time_scale, t_place, (moved, VM), dft, small],
        [planes, (1, *planes)],
        flops=2 * 10**9,
    )
    (cols_out,) = call(
        time_second_kernel,
        [((16, 136, 128), HB)],
        [time_scale, (cols_uq, VM), (received, VM), (p_cost, VM), dft, small],
        [cols, cols, cols, (16, 8, 128), planes, (1, *planes)],
        [5],
        flops=4 * 10**9,
    )
    cols_out, p_planes = lax.optimization_barrier((cols_out, p_planes))
    back = lax.all_to_all(cols_out, "ta", 0, 0)
    p_block = [
        lax.ppermute(plane, "gx", [(i, (i + d) % 8) for i in range(8)]) if d else plane
        for d, plane in enumerate(p_planes)
    ]
    (sums,) = call(sums_kernel, [((8, 8, 128), VM)], [(back[:, 128:136, :], VM)])
    sums = lax.all_to_all(sums, "gx", 0, 0)
    block_q, block_g = call(unturn_kernel, [((256, 512), VM), ((256, 512), VM)], [(back, VM)])
    (residual,) = call(
        residual_kernel,
        [((256, 512), VM)],
        [z_place, (block_q, VM)] + [(plane, VM) for plane in p_block],
    )
    (updated,) = call(
        update_kernel, [((256, 512), VM)], [(field, VM), (block_g, VM), (sums, VM)]
    )
    return updated, residual


def solution(mesh):
    placed = (P(("tile", "ta"), "gx"), P("tile"), P("tile"))
    return jax.shard_map(
        local,
        mesh=mesh,
        in_specs=placed,
        out_specs=(P(("tile", "ta"), "gx"), P(("tile", "ta"), "gx")),
        check_vma=False,
    )
```

```python
import math

import jax
import jax.numpy as jnp
import ml_dtypes
import numpy as np
from jax import lax
from jax.experimental import pallas as pl
from jax.experimental.pallas import tpu as pltpu
from jax.sharding import PartitionSpec as P

TWO_PI = 2.0 * math.pi
GRAD_EPS = 1e-06
LEN = 4096
RADIX = 32
SUB = 128
PARTS = 3
SPACE_GROUP = 32
TIME_GROUP = 16
VMEM_LIMIT = 24 * 1024 * 1024


def np_parts(values):
    rest = np.asarray(values, np.float64)
    parts = []
    for _ in range(PARTS):
        part = rest.astype(np.float32).astype(ml_dtypes.bfloat16)
        parts.append(part)
        rest = rest - part.astype(np.float64)
    return parts


def np_tables():
    j = np.arange(SUB)
    angle = TWO_PI * (np.outer(j, j) % SUB) / SUB
    cos, sin = np.cos(angle), np.sin(angle)
    dft = np.stack(np_parts(np.block([[cos, -sin], [sin, cos]])))
    k1 = np.arange(RADIX)
    twist = TWO_PI * np.outer(k1, j) / LEN
    mode = k1[:, None] + RADIX * j[None, :]
    signed = np.where(mode < LEN // 2, mode, mode - LEN)
    odd = np.where(mode == LEN // 2, 0, signed)
    small = np.stack([np.cos(twist), np.sin(twist), signed, odd]).astype(np.float32)
    return dft, small


def cadd(a, b):
    return (a[0] + b[0], a[1] + b[1])


def csub(a, b):
    return (a[0] - b[0], a[1] - b[1])


def dft4(x, sign):
    s = cadd(x[0], x[2])
    d = csub(x[0], x[2])
    t = cadd(x[1], x[3])
    e = csub(x[1], x[3])
    if sign < 0:
        ie = (e[1], -e[0])
    else:
        ie = (-e[1], e[0])
    return [cadd(s, t), cadd(d, ie), csub(s, t), csub(d, ie)]


def crot(x, turns, sign):
    turns = turns % 32
    if turns == 0:
        return x
    if turns == 8:
        return (x[1], -x[0]) if sign < 0 else (-x[1], x[0])
    c = math.cos(TWO_PI * turns / 32)
    s = sign * math.sin(TWO_PI * turns / 32)
    if turns == 4:
        return ((x[0] - sign * x[1]) * c, (x[1] + sign * x[0]) * c)
    if turns == 12:
        return ((x[0] + sign * x[1]) * c, (x[1] - sign * x[0]) * c)
    return (x[0] * c - x[1] * s, x[0] * s + x[1] * c)


def dft8(x, sign):
    even = dft4(x[0::2], sign)
    odd = [crot(value, 4 * k, sign) for k, value in enumerate(dft4(x[1::2], sign))]
    return [cadd(even[k], odd[k]) for k in range(4)] + [csub(even[k], odd[k]) for k in range(4)]


def dft32(x, sign):
    out = [None] * 32
    rows = []
    for n2 in range(8):
        y = dft4([x(8 * n1 + n2) for n1 in range(4)], sign)
        rows.append([crot(y[k1], n2 * k1, sign) for k1 in range(4)])
    for k1 in range(4):
        z = dft8([rows[n2][k1] for n2 in range(8)], sign)
        for k2 in range(8):
            out[k1 + 4 * k2] = z[k2]
    return out


def product(values, table_ref):
    parts = []
    rest = values
    for step in range(PARTS):
        part = rest.astype(jnp.bfloat16)
        parts.append(part)
        if step < PARTS - 1:
            rest = rest - part.astype(jnp.float32)
    order = [(i, k - i) for k in reversed(range(PARTS)) for i in range(k + 1)]
    left = jnp.concatenate([parts[i] for i, _ in order], axis=1)
    right = jnp.concatenate([table_ref[j] for _, j in order], axis=0)
    return jnp.dot(left, right, preferred_element_type=jnp.float32)


def transform(get, put, outputs, symbol, dft_ref, small_ref, a_ref, b_ref, group):
    re_lanes, im_lanes = slice(0, SUB), slice(SUB, 2 * SUB)

    def forward(half):
        rows = slice(8 * half, 8 * half + 8)
        planes = dft32(lambda m: get(m, half), -1)
        for k1 in range(RADIX):
            re, im = planes[k1]
            if k1:
                c = small_ref[0, k1 : k1 + 1, :]
                s = small_ref[1, k1 : k1 + 1, :]
                re, im = re * c + im * s, im * c - re * s
            a_ref[k1, rows, re_lanes] = re
            a_ref[k1, rows, im_lanes] = im

    def middle(half):
        rows = slice(8 * half, 8 * half + 8)
        for first in range(0, RADIX, group):
            ks = slice(first, first + group)
            got = product(a_ref[ks, rows].reshape(group * 8, 2 * SUB), dft_ref)
            got = got.reshape(group, 8, 2 * SUB)
            re, im = got[:, :, re_lanes], got[:, :, im_lanes]
            swapped = [
                jnp.concatenate(symbol(o, ks, re, im)[::-1], axis=2).reshape(group * 8, 2 * SUB)
                for o in range(outputs)
            ]
            got = product(jnp.concatenate(swapped, axis=0), dft_ref)
            got = got.reshape(outputs, group, 8, 2 * SUB)
            c = small_ref[0, ks][:, None, :]
            s = small_ref[1, ks][:, None, :]
            for o in range(outputs):
                im2, re2 = got[o, :, :, re_lanes], got[o, :, :, im_lanes]
                b_ref[o, ks, rows, re_lanes] = re2 * c - im2 * s
                b_ref[o, ks, rows, im_lanes] = im2 * c + re2 * s

    def inverse(half):
        rows = slice(8 * half, 8 * half + 8)
        outs = [
            dft32(lambda k: (b_ref[o, k, rows, re_lanes], b_ref[o, k, rows, im_lanes]), 1)
            for o in range(outputs)
        ]
        for m in range(RADIX):
            put(m, half, [outs[o][m] for o in range(outputs)])

    forward(0)
    forward(1)
    middle(0)
    middle(1)
    inverse(0)
    inverse(1)


def space_symbol(scale, small_ref):
    def symbol(o, ks, re, im):
        if o == 0:
            wave = small_ref[2, ks] * scale
            square = wave * wave
            even = ((square * square - square) * (1.0 / LEN))[:, None, :]
            return re * even, im * even
        odd = (small_ref[3, ks] * (scale * (1.0 / LEN)))[:, None, :]
        return -im * odd, re * odd

    return symbol


def time_symbol(scale, small_ref):
    def symbol(o, ks, re, im):
        odd = (small_ref[3, ks] * (scale * (1.0 / LEN)))[:, None, :]
        return -im * odd, re * odd

    return symbol


def row_parts(half):
    return slice(8 * half, 8 * half + 8), slice(16 + 8 * half, 24 + 8 * half)


def space_at(m):
    return m // 4, slice((m % 4) * 128, (m % 4) * 128 + 128)


def time_at(m):
    return m // 2, slice((m % 2) * 128, (m % 2) * 128 + 128)


def blocks4(tiles):
    lane = lax.broadcasted_iota(jnp.int32, tiles[0].shape, len(tiles[0].shape) - 1)
    axis = len(tiles[0].shape) - 1
    low_half = lane < 64
    even = (lane // 32) % 2 == 0

    def swap(x, y, shift, mask):
        first = jnp.where(mask, x, pltpu.roll(y, shift, axis))
        second = jnp.where(mask, pltpu.roll(x, 128 - shift, axis), y)
        return first, second

    t0, t2 = swap(tiles[0], tiles[2], 64, low_half)
    t1, t3 = swap(tiles[1], tiles[3], 64, low_half)
    t0, t1 = swap(t0, t1, 32, even)
    t2, t3 = swap(t2, t3, 32, even)
    return [t0, t1, t2, t3]


def turn_kernel(u_ref, out_ref):
    for h in range(2):
        for a in range(4):
            tile = u_ref[h * 128 : h * 128 + 128, a * 128 : a * 128 + 128].T
            out_ref[:, a * 8 : a * 8 + 8, h * 128 : h * 128 + 128] = tile.reshape(16, 8, 128)


def fold(values):
    lanes = sum(values[:, a * 128 : a * 128 + 128] for a in range(4))
    return sum(lanes[8 * a : 8 * a + 8] for a in range(4))


def space_kernel(
    scale_ref,
    place_ref,
    u_ref,
    dft_ref,
    small_ref,
    out_ref,
    *rest,
):
    p_outs = rest[:8]
    cost_ref, p_ref, v_ref, send_ref, a_ref, b_ref, sems, p_sems = rest[8:]

    def pack(ref, g, slot):
        stack = jnp.concatenate([ref[g, :, a * 128 : a * 128 + 128] for a in range(4)], axis=0)
        send_ref[g, :, 8 * slot : 8 * slot + 8, :] = stack.T.reshape(16, 8, 128)

    def get_u(m, half):
        g, cols = space_at(m)
        return tuple(u_ref[g, rows, cols] for rows in row_parts(half))

    def put_u(m, half, values):
        g, cols = space_at(m)
        for part, rows in enumerate(row_parts(half)):
            p = values[0][part] + u_ref[g, rows, cols] * values[1][part]
            p_ref[g, rows, cols] = p
            v_ref[g, rows, cols] = values[1][part]

    def get_p(m, half):
        g, cols = space_at(m)
        return tuple(p_ref[g, rows, cols] for rows in row_parts(half))

    def put_p(m, half, values):
        g, cols = space_at(m)
        for part, rows in enumerate(row_parts(half)):
            v_ref[g, rows, cols] = values[0][part] - u_ref[g, rows, cols] * values[1][part]

    symbol = space_symbol(scale_ref[0], small_ref)
    transform(get_u, put_u, 2, symbol, dft_ref, small_ref, a_ref, b_ref, SPACE_GROUP)
    copies = []
    for d in range(8):
        plane = (place_ref[0] + d) % 8
        copies.append(pltpu.make_async_copy(p_ref.at[plane], p_outs[d], p_sems.at[d]))
        copies[-1].start()
    cost_ref[...] = fold(jnp.sum(p_ref[...] * p_ref[...], axis=0))
    for g in range(8):
        pack(v_ref, g, 0)
    transform(get_p, put_p, 2, symbol, dft_ref, small_ref, a_ref, b_ref, SPACE_GROUP)
    for g in range(8):
        pack(v_ref, g, 1)
        copies.append(pltpu.make_async_copy(send_ref.at[g], out_ref.at[g], sems.at[g]))
        copies[-1].start()
    for copy in copies:
        copy.wait()


def time_first_kernel(scale_ref, place_ref, moved_ref, dft_ref, small_ref, uq_ref, a_ref, b_ref):
    for m in range(16):
        uq_ref[0, m] = moved_ref[(place_ref[0] + 4 - m // 4) % 4, (place_ref[1] + 4 - m % 4) % 4]

    def get(m, half):
        t, cols = time_at(m)
        return tuple(uq_ref[0, t, rows, cols] for rows in row_parts(half))

    def put(m, half, values):
        t, cols = time_at(m)
        for part, rows in enumerate(row_parts(half)):
            uq_ref[1, t, rows, cols] = values[0][part]

    symbol = time_symbol(scale_ref[0], small_ref)
    transform(get, put, 1, symbol, dft_ref, small_ref, a_ref, b_ref, TIME_GROUP)


def time_second_kernel(
    scale_ref,
    uq_ref,
    recv_ref,
    p_cost_ref,
    dft_ref,
    small_ref,
    out_ref,
    v_ref,
    s_ref,
    g_ref,
    sums_ref,
    a_ref,
    b_ref,
    sems,
):
    copies = []

    def send(ref, first, sem):
        for h in range(2):
            lanes = slice(h * 128, h * 128 + 128)
            rows = slice(first + 32 * h, first + 32 * h + 32)
            copies.append(
                pltpu.make_async_copy(ref.at[:, :, lanes], out_ref.at[:, rows, :], sems.at[sem + h])
            )
            copies[-1].start()

    send(uq_ref.at[1], 0, 0)
    costs = [jnp.zeros((8, 128), jnp.float32)] * 8
    for m in range(16):
        for h in range(2):
            cols = slice(h * 128, h * 128 + 128)
            for o, ref in enumerate((v_ref, g_ref)):
                tiles = blocks4([recv_ref[(4 * h + k) * 16 + m, 8 * o : 8 * o + 8] for k in range(4)])
                for a in range(4):
                    rows = slice(8 * a, 8 * a + 8)
                    ref[m, rows, cols] = tiles[a]
                    if o == 0:
                        q = uq_ref[1, m, rows, cols]
                        w = uq_ref[0, m, rows, cols] * tiles[a]
                        s_ref[m, rows, cols] = q + w
                        costs[4 * h + a] = costs[4 * h + a] + q * (0.5 * q + w)

    def get_v(m, half):
        t, cols = time_at(m)
        return tuple(v_ref[t, rows, cols] for rows in row_parts(half))

    def put_v(m, half, values):
        t, cols = time_at(m)
        for part, rows in enumerate(row_parts(half)):
            v_ref[t, rows, cols] = (
                g_ref[t, rows, cols] - uq_ref[0, t, rows, cols] * values[0][part]
            )

    norms = [jnp.zeros((8, 128), jnp.float32)] * 8

    def get_s(m, half):
        t, cols = time_at(m)
        return tuple(s_ref[t, rows, cols] for rows in row_parts(half))

    def put_s(m, half, values):
        t, cols = time_at(m)
        for part, rows in enumerate(row_parts(half)):
            g = v_ref[t, rows, cols] - values[0][part]
            g_ref[t, rows, cols] = g
            slot = 2 * (m % 4) + part
            norms[slot] = norms[slot] + g * g

    symbol = time_symbol(scale_ref[0], small_ref)
    transform(get_v, put_v, 1, symbol, dft_ref, small_ref, a_ref, b_ref, TIME_GROUP)
    transform(get_s, put_s, 1, symbol, dft_ref, small_ref, a_ref, b_ref, TIME_GROUP)
    send(g_ref, 64, 2)
    cost = sum(costs) + 0.5 * p_cost_ref[...]
    norm = sum(norms)
    both = jnp.concatenate([cost[0:4] + cost[4:8], norm[0:4] + norm[4:8]], axis=0)
    sums_ref[...] = jnp.broadcast_to(both[None], (16, 8, 128))
    copies.append(pltpu.make_async_copy(sums_ref, out_ref.at[:, 128:136, :], sems.at[4]))
    copies[-1].start()
    for copy in copies:
        copy.wait()


def sums_kernel(recv_ref, out_ref):
    total = jnp.sum(recv_ref[...], axis=0)
    cost = jnp.sum(total[0:4], axis=0, keepdims=True)
    norm = jnp.sum(total[4:8], axis=0, keepdims=True)
    row = lax.broadcasted_iota(jnp.int32, (8, 128), 0)
    out_ref[...] = jnp.broadcast_to(jnp.where(row == 0, cost, norm)[None], (8, 8, 128))


def unturn(recv_ref, first, ref):
    for h in range(2):
        for a in range(4):
            rows = slice(first + 32 * h + 8 * a, first + 32 * h + 8 * a + 8)
            tile = recv_ref[:, rows, :]
            ref[h * 128 : h * 128 + 128, a * 128 : a * 128 + 128] = tile.reshape(128, 128).T


def unturn_kernel(recv_ref, q_ref, g_ref):
    unturn(recv_ref, 0, q_ref)
    unturn(recv_ref, 64, g_ref)


def residual_kernel(place_ref, q_ref, *refs):
    r_ref = refs[8]
    for d in range(8):
        rows = pl.ds(pl.multiple_of((place_ref[0] + 8 - d) % 8 * 32, 32), 32)
        r_ref[rows, :] = q_ref[rows, :] + refs[d][...]


def update_kernel(u_ref, g_ref, sums_ref, out_ref, new_ref, sems):
    sums = jnp.sum(sums_ref[...], axis=0)
    cost = jnp.sum(sums[0:1, :], axis=1, keepdims=True)
    norm = jnp.sum(sums[1:2, :], axis=1, keepdims=True)
    step = cost / (norm + GRAD_EPS)
    copies = []
    for part in range(4):
        rows = slice(64 * part, 64 * part + 64)
        new_ref[rows, :] = u_ref[rows, :] - step * g_ref[rows, :]
        copies.append(
            pltpu.make_async_copy(new_ref.at[rows, :], out_ref.at[rows, :], sems.at[part])
        )
        copies[-1].start()
    for copy in copies:
        copy.wait()


VM = pl.BlockSpec(memory_space=pltpu.VMEM)
SM = pl.BlockSpec(memory_space=pltpu.SMEM)
HB = pl.BlockSpec(memory_space=pl.ANY)


def f32(*shape):
    return jax.ShapeDtypeStruct(shape, jnp.float32)


def call(kernel, outs, ins, scratch=(), sems=(), flops=0):
    return pl.pallas_call(
        kernel,
        out_shape=[f32(*shape) for shape, _ in outs],
        in_specs=[spec for _, spec in ins],
        out_specs=[spec for _, spec in outs],
        scratch_shapes=[pltpu.VMEM(shape, jnp.float32) for shape in scratch]
        + [pltpu.SemaphoreType.DMA((count,)) for count in sems],
        cost_estimate=pl.CostEstimate(flops=flops, bytes_accessed=2**21, transcendentals=0),
        compiler_params=pltpu.CompilerParams(vmem_limit_bytes=VMEM_LIMIT),
    )(*[array for array, _ in ins])


def shift_pairs(axis, shift):
    pairs = []
    for y in range(4):
        for x in range(4):
            to = (y, (x + shift) % 4) if axis else ((y + shift) % 4, x)
            pairs.append((4 * y + x, 4 * to[0] + to[1]))
    return pairs


def along_x(turned, x):
    pieces = turned.reshape(4, 4, 32, 256)
    moved = []
    for d in range(4):
        piece = lax.dynamic_index_in_dim(pieces, (x + d) % 4, 1, keepdims=False)
        moved.append(lax.ppermute(piece, "ta", shift_pairs(1, d)) if d else piece)
    return moved


def along_y(pieces, y):
    moved = []
    for e in range(4):
        piece = jnp.stack(
            [lax.dynamic_index_in_dim(part, (y + e) % 4, 0, keepdims=False) for part in pieces]
        )
        moved.append(lax.ppermute(piece, "ta", shift_pairs(0, e)) if e else piece)
    return jnp.stack(moved)


def local(field, time_period, space_period):
    dft_np, small_np = np_tables()
    dft = (jnp.asarray(dft_np), VM)
    small = (jnp.asarray(small_np), VM)
    time_scale = (TWO_PI / time_period, SM)
    space_scale = (TWO_PI / space_period, SM)
    rows, cols = (8, 32, 512), (16, 32, 256)
    planes = (RADIX, 16, 2 * SUB)
    here = lax.axis_index("ta")
    y, x = here // 4, here % 4
    z = lax.axis_index("gx")
    z_place = (z.reshape(1), SM)
    t_place = (jnp.stack([y, x]), SM)

    rows_u = lax.all_to_all(field.reshape(rows), "gx", 0, 0)
    (turned,) = call(turn_kernel, [(cols, VM)], [(field, VM)])
    first_move = along_x(turned, x)
    pieces, *p_planes, p_cost = call(
        space_kernel,
        [((8, 16, 16, 128), HB)] + [((32, 512), HB)] * 8 + [((8, 128), VM)],
        [space_scale, z_place, (rows_u, VM), dft, small],
        [rows, rows, (8, 16, 16, 128), planes, (2, *planes)],
        [8, 8],
        flops=8 * 10**9,
    )
    pieces, first_move = lax.optimization_barrier((pieces, first_move))
    received = lax.all_to_all(pieces.reshape(128, 16, 128), ("gx", "ta"), 0, 0)
    moved = along_y(first_move, y)
    (cols_uq,) = call(
        time_first_kernel,
        [((2, *cols), VM)],
        [time_scale, t_place, (moved, VM), dft, small],
        [planes, (1, *planes)],
        flops=2 * 10**9,
    )
    (cols_out,) = call(
        time_second_kernel,
        [((16, 136, 128), HB)],
        [time_scale, (cols_uq, VM), (received, VM), (p_cost, VM), dft, small],
        [cols, cols, cols, (16, 8, 128), planes, (1, *planes)],
        [5],
        flops=4 * 10**9,
    )
    cols_out, p_planes = lax.optimization_barrier((cols_out, p_planes))
    back = lax.all_to_all(cols_out, "ta", 0, 0)
    p_block = [
        lax.ppermute(plane, "gx", [(i, (i + d) % 8) for i in range(8)]) if d else plane
        for d, plane in enumerate(p_planes)
    ]
    (sums,) = call(sums_kernel, [((8, 8, 128), VM)], [(back[:, 128:136, :], VM)])
    sums = lax.all_to_all(sums, "gx", 0, 0)
    block_q, block_g = call(unturn_kernel, [((256, 512), VM), ((256, 512), VM)], [(back, VM)])
    (residual,) = call(
        residual_kernel,
        [((256, 512), VM)],
        [z_place, (block_q, VM)] + [(plane, VM) for plane in p_block],
    )
    (updated,) = call(
        update_kernel,
        [((256, 512), HB)],
        [(field, VM), (block_g, VM), (sums, VM)],
        [(256, 512)],
        [4],
    )
    return updated, residual


def solution(mesh):
    placed = (P(("tile", "ta"), "gx"), P("tile"), P("tile"))
    return jax.shard_map(
        local,
        mesh=mesh,
        in_specs=placed,
        out_specs=(P(("tile", "ta"), "gx"), P(("tile", "ta"), "gx")),
        check_vma=False,
    )
```
